32 devices in a mesh: groups: 2 (over y), blocks: 4 (over z), tiles: 2 (over x), sub: 2 (over core).
Axes of the slice: x: 2, y: 2, z: 4, core: 2. Of those that a mesh axis runs over, the one named last changes fastest.
Arguments:
- seg_feat: bfloat16 [8, 4, 2048, 128], P(('groups', 'tiles', 'sub'), 'blocks'), parts along dimension 0, may hold values from -6 to 6
- seg_block: int32 [8, 4, 2048, 1], P(('groups', 'tiles', 'sub'), 'blocks'), parts along dimension 0, may hold values from 0 to 3; in each aligned block of 2048 rows (0 to 2047, 2048 to 4095, ..., all dimensions but the last counted through in order) at most 1024 rows name the same one
- depth_rank: int32 [8, 4, 8, 256], P(('groups', 'tiles', 'sub'), 'blocks'), parts along dimension 0, may hold values from 0 to 7, as said below
- w_in: bfloat16 [4, 128, 512], P('blocks'), may hold values from -0.5 to 0.5
- w_hidden: bfloat16 [4, 4, 512, 512], P('blocks'), may hold values from -0.25 to 0.25
- w_out: bfloat16 [4, 512, 128], P('blocks'), may hold values from -0.25 to 0.25
- w_dens: bfloat16 [4, 512], P('blocks'), may hold values from -0.25 to 0.25
- conv_w: bfloat16 [3, 3, 3, 128, 128], replicated, may hold values from -0.1875 to 0.1875
Outputs:
- decoded: bfloat16 [128, 64, 128], P(('groups', 'tiles', 'sub'), 'blocks'), parts along dimension 0
The draws below stay inside these ranges and needn't reach their ends.
There are 2 independent parts, one for each index of `groups`. The reference program is written for one: setup_inputs(seed, part) draws one part's arguments, and reference() takes and returns one part's arrays. A program takes and returns all parts, laid end to end along the dimension named above; an argument that names none is the same for every part. Nothing has to cross between parts.
Inputs may be any that keep to these rules, and one draw needn't show every extreme that they name: `seg_block`: among one device's 2048 segments, no block is named more than 1024 times; some device names some block exactly 1024 times. `depth_rank`: for every ray, its 8 segments' ranks are a permutation of 0 .. 7.
All inputs are finite; a program needn't handle non-finite values.
Results may differ from the reference program's by a relative error of at most 0.02.
Values may be sent and summed in bfloat16 or wider, within the bound.
A program may use at most 64 MiB of HBM per device.

```python
import math
import jax
import jax.numpy as jnp
import numpy as np
from jax import lax

F_IN = 128
HID = 512
FEAT = 128
LAYERS = 4
SEGS_RAY = 8
CONV_LAYERS = 3
TW = 16
TH = 16
RAYS_DEV = 256
SEG_DEV = 2048
CAP = 1024
RT = 4
N_BLOCKS = 4


def draw_depth_rank(key, part):
    scores = jax.random.randint(key, (RT, N_BLOCKS, SEGS_RAY, RAYS_DEV), 0, 1 << 20) * SEGS_RAY
    scores = scores + jnp.arange(SEGS_RAY, dtype=jnp.int32)[:, None]
    ordering = jnp.argsort(scores, axis=2)
    return jnp.argsort(ordering, axis=2).astype(jnp.int32)


def steps_of(rng, shape, split, smallest, largest):
    def one(axis_at, blocks):
        steps = jax.random.uniform(jax.random.fold_in(jax.random.fold_in(rng, 6), axis_at), (blocks,), jnp.float32, smallest / len(split), largest / len(split))
        return jnp.repeat(jnp.exp(steps), shape[axis_at] // blocks).reshape((-1,) + (1,) * (len(shape) - axis_at - 1))

    gain = one(*split[0])
    for cut in split[1:]:
        gain = gain * one(*cut)
    return gain


def deal_out(rng, own, number, rows, amount, top, most, skew):
    ranking = jax.random.permutation(rng, amount)
    crowded, usual = load_shares(amount, rows * top, most, skew, True), load_shares(amount, rows * top, most, skew, False)
    places = jnp.arange(amount)

    def named(lengths, turn):
        used = int((lengths > 0).sum())
        fixed = max(1, used // 4)
        shifted = fixed + (places - fixed + turn * (used - fixed)) % max(1, amount - fixed)
        return jnp.zeros((amount,), jnp.int32).at[ranking[jnp.where(places < fixed, places, shifted)]].set(jnp.asarray(lengths, jnp.int32))

    lengths = jnp.where(number % 4 == 0, named(crowded, number // 4), named(usual, number - number // 4 - 1))
    mixed = jax.random.permutation(jax.random.fold_in(own, 3), amount)
    donor, receiver = mixed[0:amount // 2 * 2:2], mixed[1:amount // 2 * 2:2]
    slack = jnp.minimum(lengths[donor] - 1, most - lengths[receiver]) // 2
    slack = jnp.where((donor == ranking[0]) | (receiver == ranking[0]) | (lengths[receiver] == 0), 0, jnp.maximum(slack, 0))
    shifted = jax.random.randint(jax.random.fold_in(own, 4), (amount // 2,), 0, 1 << 20) % (slack + 1)
    lengths = lengths.at[donor].add(-shifted).at[receiver].add(shifted)
    labels = jnp.searchsorted(jnp.cumsum(lengths), jnp.arange(rows * top), side="right").astype(jnp.int32)
    grid = labels.reshape(top, rows).T
    grid = grid[jax.random.permutation(jax.random.fold_in(own, 1), rows)]
    turn = jax.random.randint(jax.random.fold_in(own, 2), (rows, 1), 0, top)
    return jnp.take_along_axis(grid, (jnp.arange(top)[None, :] + turn) % top, axis=1)


def load_shares(count, total, most, lean, full):
    portions = [(1 << 20) // math.isqrt(grade ** lean) + 1 for grade in range(1, count + 1)]
    largest = most if full else min(most, max(-(-total // count), total * portions[0] // sum(portions)))
    least = 1 if total - largest >= count - 1 else 0
    holding, spare = [largest] + [least] * (count - 1), total - largest - least * (count - 1)
    while spare > 0:
        free = [i for i in range(1, count) if holding[i] < largest] or [i for i in range(1, count) if holding[i] < most]
        mass, remaining = sum([portions[i] for i in free]), spare
        for i in free:
            extra = min(most - holding[i], max(1, remaining * portions[i] // mass), spare)
            holding[i] = holding[i] + extra
            spare = spare - extra
    return np.array(holding)


def noise(stream_key, shape, deviation, most, cuts=(), kind=jnp.bfloat16):
    factor_of = steps_of(stream_key, shape, cuts, -0.22, 0.18) if cuts else 1.0
    entries = jax.random.normal(stream_key, shape, jnp.float32) * deviation * factor_of
    return jnp.minimum(jnp.maximum(entries, -most), most).astype(kind)


def setup_inputs(seed: int = 0, part: int = 0) -> dict:
    key_of = jax.random.split(jax.random.key(seed), 9)
    part_keys = jax.random.split(jax.random.fold_in(key_of[8], part), 9)
    seg_feat = noise(part_keys[0], (RT, N_BLOCKS, SEG_DEV, F_IN), 1.0, 6.0, ((0, 4), (1, 4)))
    seg_block_keys = jax.random.split(jax.random.fold_in(part_keys[1], 1), RT * N_BLOCKS * SEG_DEV // SEG_DEV)
    seg_block_turns = jax.random.permutation(jax.random.fold_in(part_keys[1], 3), RT * N_BLOCKS * SEG_DEV // SEG_DEV)
    seg_block = jax.vmap(lambda own, number: deal_out(jax.random.fold_in(part_keys[1], 2), own, number, SEG_DEV, N_BLOCKS, 1, CAP, 2))(seg_block_keys, seg_block_turns).reshape((RT, N_BLOCKS, SEG_DEV, 1))
    depth_rank = draw_depth_rank(jax.random.fold_in(jax.random.fold_in(key_of[8], part), 71), part)
    w_in = noise(key_of[3], (N_BLOCKS, F_IN, HID), F_IN ** -0.5, 0.5, ((0, 4),))
    w_hidden = noise(key_of[4], (N_BLOCKS, LAYERS, HID, HID), HID ** -0.5, 0.25, ((0, 4),))
    w_out = noise(key_of[5], (N_BLOCKS, HID, FEAT), HID ** -0.5, 0.25, ((0, 4),))
    w_dens = noise(key_of[6], (N_BLOCKS, HID), HID ** -0.5, 0.25, ((0, 4),))
    conv_w = noise(key_of[7], (CONV_LAYERS, 3, 3, FEAT, FEAT), (9 * FEAT) ** -0.5, 0.1875)
    return dict(seg_feat=seg_feat, seg_block=seg_block, depth_rank=depth_rank, w_in=w_in, w_hidden=w_hidden, w_out=w_out, w_dens=w_dens, conv_w=conv_w)


def place_rows(block_ids, capacity, block_count):
    onehot = (block_ids[:, None] == jnp.arange(block_count, dtype=jnp.int32)[None, :]).astype(jnp.int32)
    before = jnp.cumsum(onehot, axis=0) - onehot
    return (block_ids * capacity + jnp.sum(before * onehot, axis=1)).astype(jnp.int32)


def evaluate(row_block, first_weight, hidden, last_weight, density_row):
    hidden_act = jax.nn.silu(jnp.dot(row_block, first_weight, preferred_element_type=jnp.float32)).astype(jnp.bfloat16)
    for layer_index in range(hidden.shape[0]):
        update = jax.nn.silu(jnp.dot(hidden_act, hidden[layer_index], preferred_element_type=jnp.float32))
        hidden_act = (hidden_act.astype(jnp.float32) + update).astype(jnp.bfloat16)
    features = jnp.dot(hidden_act, last_weight, preferred_element_type=jnp.float32).astype(jnp.bfloat16)
    raw_density = jnp.dot(hidden_act, density_row, preferred_element_type=jnp.float32)
    density = (0.25 * jax.nn.softplus(raw_density)).astype(jnp.bfloat16)
    return features, density


def composite(features, density, rank_table):
    density_f32 = density.astype(jnp.float32)
    in_front = (rank_table[:, None, :] < rank_table[None, :, :]).astype(jnp.float32)
    optical = jnp.sum(density_f32[:, None, :] * in_front, axis=0)
    weight = jnp.exp(-optical) * (1.0 - jnp.exp(-density_f32))
    pixel_color = jnp.sum(weight[:, :, None] * features.astype(jnp.float32), axis=0)
    return pixel_color.astype(jnp.bfloat16)


def conv_layer(padded, kernel, out_rows, out_cols):
    pieces = []
    for offset_y in range(3):
        for offset_x in range(3):
            pieces.append(padded[offset_y:offset_y + out_rows, offset_x:offset_x + out_cols])
    patches = jnp.concatenate(pieces, axis=-1)
    channels = kernel.shape[-1]
    result = jnp.dot(patches, kernel.reshape(9 * kernel.shape[2], channels), preferred_element_type=jnp.float32)
    center = padded[1:1 + out_rows, 1:1 + out_cols].astype(jnp.float32)
    return (center + jax.nn.silu(result)).astype(jnp.bfloat16)


def reference(seg_feat, seg_block, depth_rank, w_in, w_hidden, w_out, w_dens, conv_w):
    block_table = seg_block[..., 0]
    slot_index = jax.vmap(jax.vmap(lambda block_ids: place_rows(block_ids, CAP, N_BLOCKS)))(block_table)

    def fill_rows(row_block, positions):
        return jnp.zeros((N_BLOCKS * CAP, F_IN), jnp.bfloat16).at[positions].set(row_block)

    sendbuf = jax.vmap(jax.vmap(fill_rows))(seg_feat, slot_index).reshape(RT, N_BLOCKS, N_BLOCKS, CAP, F_IN)

    def per_block(block_id):
        row_block = sendbuf[:, :, block_id].reshape(RT * N_BLOCKS * CAP, F_IN)
        features, density = evaluate(row_block, w_in[block_id], w_hidden[block_id], w_out[block_id], w_dens[block_id])
        return features.reshape(RT, N_BLOCKS, CAP, FEAT), density.reshape(RT, N_BLOCKS, CAP)

    feat_all, density_all = lax.map(per_block, jnp.arange(N_BLOCKS, dtype=jnp.int32))
    feat_back = feat_all.transpose(1, 2, 0, 3, 4).reshape(RT, N_BLOCKS, N_BLOCKS * CAP, FEAT)
    density_back = density_all.transpose(1, 2, 0, 3).reshape(RT, N_BLOCKS, N_BLOCKS * CAP)

    def finish(feat_rows, density_rows, positions, rank_table):
        feat_seg = feat_rows[positions].reshape(SEGS_RAY, RAYS_DEV, FEAT)
        density_seg = density_rows[positions].reshape(SEGS_RAY, RAYS_DEV)
        return composite(feat_seg, density_seg, rank_table)

    colors = jax.vmap(jax.vmap(finish))(feat_back, density_back, slot_index, depth_rank)
    image_map = colors.reshape(RT, N_BLOCKS, TH, TW, FEAT).transpose(0, 2, 1, 3, 4).reshape(RT * TH, N_BLOCKS * TW, FEAT)
    for layer_index in range(CONV_LAYERS):
        padded = jnp.pad(image_map, ((1, 1), (1, 1), (0, 0)))
        image_map = conv_layer(padded, conv_w[layer_index], RT * TH, N_BLOCKS * TW)
    return image_map
```

```python
import functools

import jax
import jax.numpy as jnp
from jax import lax
from jax.experimental import pallas as pl
from jax.experimental.pallas import tpu as pltpu
from jax.sharding import PartitionSpec as P

SEGS_RAY = 8
CONV_LAYERS = 3
TW = 16
TH = 16
RAYS_DEV = 256
MESH = pl.DeviceIdType.MESH
F32 = jnp.float32
BF16 = jnp.bfloat16


def silu(value):
    half = 0.5 * value
    return half + half * jnp.tanh(half)


def softplus(value):
    return jnp.maximum(value, 0.0) + jnp.log1p(jnp.exp(-jnp.abs(value)))


def block_at(step, place, count):
    near = jnp.minimum(place, count - 1 - place)
    distance = (step + 1) // 2
    paired = jnp.where(step % 2 == 1, place + distance, place - distance)
    rest = jnp.where(2 * place <= count - 1, step, count - 1 - step)
    return jnp.where(step <= 2 * near, paired, rest)


Z, X, Y, D, SA, SX, SY, SD, ZD = range(9)


def render_kernel(
    count,
    capacity,
    row_tile,
    feat_ref,
    block_ref,
    rank_ref,
    w_in_ref,
    w_hid_ref,
    w_out_ref,
    w_dens_ref,
    color_ref,
    hid,
    ends,
    slot_row,
    slot_col,
    rank_col,
    act,
    heads,
    total,
    send_sem,
    recv_sem,
    ends_send,
    ends_recv,
    own_sem,
):
    place = lax.axis_index("blocks")
    tile = lax.axis_index("tiles")
    group = lax.axis_index("groups")
    core = lax.axis_index("sub")
    tile_mate = tile + 1 - 2 * (tile % 2)
    group_mate = group + 1 - 2 * (group % 2)
    core_mate = 1 - core
    tx, gy = tile % 2, group % 2
    layers = w_hid_ref.shape[0]
    hidden = w_hid_ref.shape[2]
    part = hidden // 8
    end_rows = ends.shape[1]
    end_half = end_rows // 2
    feats = w_out_ref.shape[1]
    in_width = w_in_ref.shape[0]
    segments = feat_ref.shape[0]

    def eighth(a, b, c):
        return (a * 2 + b) * 2 + c

    to_x, to_y, to_c = {"tiles": tile_mate}, {"groups": group_mate}, {"sub": core_mate}

    barrier = pltpu.get_barrier_semaphore()
    pl.semaphore_signal(barrier, inc=1, device_id=to_x, device_id_type=MESH)
    pl.semaphore_signal(barrier, inc=1, device_id=to_y, device_id_type=MESH)
    pl.semaphore_signal(barrier, inc=1, device_id=to_c, device_id_type=MESH)

    @pl.when(place > 0)
    def _():
        pl.semaphore_signal(barrier, inc=1, device_id={"blocks": place - 1}, device_id_type=MESH)

    @pl.when(place < count - 1)
    def _():
        pl.semaphore_signal(barrier, inc=1, device_id={"blocks": place + 1}, device_id_type=MESH)

    own = pltpu.make_async_copy(w_hid_ref, hid.at[place], own_sem)
    own.start()
    ends[place, 0:in_width] = w_in_ref[...]
    ends[place, in_width : in_width + feats] = w_out_ref[...].T
    ends[place, in_width + feats : end_rows] = jnp.broadcast_to(
        w_dens_ref[...], (end_rows - in_width - feats, hidden)
    )
    own.wait()

    peers = 3 + jnp.minimum(place, 1) + jnp.minimum(count - 1 - place, 1)
    pl.semaphore_wait(barrier, peers)

    def piece(block, layer, which):
        return hid.at[block, layer, pl.ds(pl.multiple_of(which * part, part), part)]

    def move(block, layer, which, kind, target, send_kind=None):
        ref = piece(block, layer, which)
        return pltpu.make_async_remote_copy(
            src_ref=ref,
            dst_ref=ref,
            send_sem=send_sem.at[block, layer, kind if send_kind is None else send_kind],
            recv_sem=recv_sem.at[block, layer, kind],
            device_id=target,
            device_id_type=MESH,
        )

    def move_ends(block, half, kind, target, send_kind=None):
        ref = ends.at[block, pl.ds(pl.multiple_of(half * end_half, end_half), end_half)]
        return pltpu.make_async_remote_copy(
            src_ref=ref,
            dst_ref=ref,
            send_sem=ends_send.at[block, kind if send_kind is None else send_kind],
            recv_sem=ends_recv.at[block, kind],
            device_id=target,
            device_id_type=MESH,
        )

    e_own = eighth(tx, gy, core)
    e_x = eighth(1 - tx, gy, core)
    e_y = eighth(tx, 1 - gy, core)
    e_d = eighth(1 - tx, 1 - gy, core)
    m_own = eighth(tx, gy, core_mate)
    m_x = eighth(1 - tx, gy, core_mate)
    m_y = eighth(tx, 1 - gy, core_mate)
    m_d = eighth(1 - tx, 1 - gy, core_mate)
    up, down = {"blocks": place + 1}, {"blocks": place - 1}

    def own_up(action):
        @pl.when(place < count - 1)
        def _():
            action(move_ends(place, core, 0, up))
            for layer in range(layers):
                action(move(place, layer, e_own, Z, up))

    def own_down(action):
        @pl.when(place > 0)
        def _():
            action(move_ends(place, core, 0, down, 2))
            for layer in range(layers):
                action(move(place, layer, e_own, Z, down, ZD))

    own_up(lambda c: c.start())
    own_down(lambda c: c.start())

    def onward(block, action):
        @pl.when((block < place) & (place < count - 1))
        def _():
            action(up)

        @pl.when((block > place) & (place > 0))
        def _():
            action(down)

    def arrive(block, layer):
        move(block, layer, e_own, Z, up).wait_recv()
        onward(block, lambda to: move(block, layer, e_own, Z, to).start())
        move(block, layer, e_own, X, to_x).start()
        move(block, layer, e_own, Y, to_y).start()
        move(block, layer, e_own, SA, to_c).start()

    def arrive_ends(block):
        move_ends(block, core, 0, up).wait_recv()
        onward(block, lambda to: move_ends(block, core, 0, to).start())
        move_ends(block, core, 1, to_c).start()

    def cross(block, layer):
        move(block, layer, e_x, X, to_x).wait_recv()
        move(block, layer, e_y, Y, to_y).wait_recv()

        @pl.when(core == 0)
        def _():
            move(block, layer, e_x, D, to_y).start()

        @pl.when(core == 1)
        def _():
            move(block, layer, e_y, D, to_x).start()

        move(block, layer, e_x, SX, to_c).start()
        move(block, layer, e_y, SY, to_c).start()

    def corner(block, layer):
        move(block, layer, e_d, D, to_x).wait_recv()
        move(block, layer, e_d, SD, to_c).start()

    def ready(block, layer):
        move(block, layer, m_own, SA, to_c).wait_recv()
        move(block, layer, m_x, SX, to_c).wait_recv()
        move(block, layer, m_y, SY, to_c).wait_recv()
        move(block, layer, m_d, SD, to_c).wait_recv()

    def item(step, layer, ahead):
        return step + (layer + ahead) // layers, (layer + ahead) % layers

    def exchange(step, layer):
        for ahead, action in ((3, arrive), (2, cross), (1, corner)):
            later, its_layer = item(step, layer, ahead)

            @pl.when((later > 0) & (later < count))
            def _():
                block = block_at(later, place, count)
                if action is arrive and its_layer == 0:
                    arrive_ends(block)
                action(block, its_layer)

    rows16 = 16
    lane = lax.broadcasted_iota(jnp.int32, (128, 128), 1)
    sub = lax.broadcasted_iota(jnp.int32, (128, 128), 0)
    earlier = (sub < lane).astype(F32).astype(BF16)
    names = lax.broadcasted_iota(jnp.int32, (rows16, 128), 0)
    base = names.astype(F32) * capacity
    carry = jnp.zeros((rows16, 1), F32)
    for chunk in range(segments // 128):
        cols = slice(chunk * 128, (chunk + 1) * 128)
        named = (jnp.broadcast_to(block_ref[:, cols], (rows16, 128)) == names).astype(F32)
        before = jnp.dot(named.astype(BF16), earlier, preferred_element_type=F32) + carry
        carry = carry + jnp.sum(named, axis=1, keepdims=True)
        slots = jnp.sum(named * (before + base), axis=0, keepdims=True)
        slot_row[:, cols] = slots.astype(jnp.int32)
        slot_col[cols, :] = jnp.broadcast_to(slots, (128, 128)).T.astype(jnp.int32)
    for k in range(SEGS_RAY):
        spread = jnp.broadcast_to(rank_ref[k : k + 1, :].astype(F32), (128, RAYS_DEV))
        rank_col[k] = spread.T
    total[...] = jnp.zeros_like(total)

    tiles_n = capacity // row_tile

    def tile_loop(body):
        def run(index, carry_in):
            body(pl.ds(pl.multiple_of(index * row_tile, row_tile), row_tile), index)
            return carry_in

        lax.fori_loop(0, tiles_n, run, 0)

    def gather_in(block):
        def body(rows, index):
            wanted = (
                lax.broadcasted_iota(jnp.int32, (row_tile, segments), 0)
                + block * capacity
                + index * row_tile
            )
            pick = (slot_row[...] == wanted).astype(F32).astype(BF16)
            mine = jnp.dot(pick, feat_ref[...], preferred_element_type=F32).astype(BF16)
            act[rows] = silu(
                jnp.dot(mine, ends[block, 0:in_width], preferred_element_type=F32)
            ).astype(BF16)

        tile_loop(body)

    def layer_step(block, layer):
        def body(rows, index):
            value = act[rows]
            update = silu(jnp.dot(value, hid[block, layer], preferred_element_type=F32))
            act[rows] = (value.astype(F32) + update).astype(BF16)

        tile_loop(body)

    def head_step(block):
        w_feat = ends[block, in_width : in_width + feats]
        w_den = jnp.broadcast_to(ends[block, in_width + feats : in_width + feats + 1], (128, hidden))
        contract = (((1,), (1,)), ((), ()))

        def body(rows, index):
            value = act[rows]
            heads[rows, 0:feats] = lax.dot_general(
                value, w_feat, contract, preferred_element_type=F32
            ).astype(BF16)
            raw = lax.dot_general(value, w_den, contract, preferred_element_type=F32)
            heads[rows, feats : feats + 128] = (0.25 * softplus(raw)).astype(BF16)

        tile_loop(body)

    def scatter_back(block):
        def run(index, carry_in):
            rows = pl.ds(pl.multiple_of(index * 256, 256), 256)
            held = slot_col[rows] - block * capacity
            columns = lax.broadcasted_iota(jnp.int32, (256, 128), 1)
            pick = jnp.concatenate(
                [
                    (held == columns + 128 * j).astype(F32).astype(BF16)
                    for j in range(capacity // 128)
                ],
                axis=1,
            )
            total[rows] += jnp.dot(pick, heads[...], preferred_element_type=F32)
            return carry_in

        lax.fori_loop(0, segments // 256, run, 0)

    def step_body(step, carry_in):
        block = block_at(step, place, count)
        for layer in range(layers):
            exchange(step, layer)

            @pl.when(step > 0)
            def _():
                if layer == 0:
                    move_ends(block, core_mate, 1, to_c).wait_recv()
                ready(block, layer)

            if layer == 0:
                gather_in(block)
            layer_step(block, layer)
        head_step(block)
        scatter_back(block)
        return carry_in

    lax.fori_loop(0, count, step_body, 0)

    density = [total[k * RAYS_DEV : (k + 1) * RAYS_DEV, feats : feats + 128] for k in range(SEGS_RAY)]
    color = jnp.zeros((RAYS_DEV, feats), F32)
    for k in range(SEGS_RAY):
        optical = jnp.zeros((RAYS_DEV, 128), F32)
        for j in range(SEGS_RAY):
            if j != k:
                optical += jnp.where(rank_col[j] < rank_col[k], density[j], 0.0)
        weight = jnp.exp(-optical) * (1.0 - jnp.exp(-density[k]))
        color += weight * total[k * RAYS_DEV : (k + 1) * RAYS_DEV, 0:feats]
    color_ref[...] = color.astype(BF16)

    own_up(lambda c: c.wait_send())
    own_down(lambda c: c.wait_send())

    def drain(step, carry_in):
        block = block_at(step, place, count)
        onward(block, lambda to: move_ends(block, core, 0, to).wait_send())
        move_ends(block, core, 1, to_c).wait_send()
        for layer in range(layers):
            onward(block, lambda to, layer=layer: move(block, layer, e_own, Z, to).wait_send())
            for kind in (X, Y, D, SA, SX, SY, SD):
                move(block, layer, e_own, kind, to_c).wait_send()
        return carry_in

    lax.fori_loop(1, count, drain, 0)


def render(count, rows, block_ids, ranks, w_in, w_hid, w_out, w_dens):
    segments, in_width = rows.shape
    capacity = 2 * segments // count
    layers, hidden, _ = w_hid.shape
    feats = w_out.shape[1]
    row_tile = min(512, capacity)
    end_rows = in_width + feats + 32
    vmem = pl.BlockSpec(memory_space=pltpu.VMEM)
    macs = count * capacity * hidden * (in_width + layers * hidden + feats)
    return pl.pallas_call(
        functools.partial(render_kernel, count, capacity, row_tile),
        out_shape=jax.ShapeDtypeStruct((RAYS_DEV, feats), BF16),
        in_specs=[vmem, vmem, vmem, vmem, pl.BlockSpec(memory_space=pl.ANY), vmem, vmem],
        out_specs=vmem,
        scratch_shapes=[
            pltpu.VMEM((count, layers, hidden, hidden), BF16),
            pltpu.VMEM((count, end_rows, hidden), BF16),
            pltpu.VMEM((1, segments), jnp.int32),
            pltpu.VMEM((segments, 128), jnp.int32),
            pltpu.VMEM((SEGS_RAY, RAYS_DEV, 128), F32),
            pltpu.VMEM((capacity, hidden), BF16),
            pltpu.VMEM((capacity, feats + 128), BF16),
            pltpu.VMEM((segments, feats + 128), F32),
            pltpu.SemaphoreType.DMA((count, layers, 9)),
            pltpu.SemaphoreType.DMA((count, layers, 8)),
            pltpu.SemaphoreType.DMA((count, 3)),
            pltpu.SemaphoreType.DMA((count, 2)),
            pltpu.SemaphoreType.DMA,
        ],
        compiler_params=pltpu.CompilerParams(
            collective_id=0, has_side_effects=True, vmem_limit_bytes=56 * 1024 * 1024
        ),
        cost_estimate=pl.CostEstimate(flops=2 * macs, bytes_accessed=4 << 20, transcendentals=0),
        name="render",
    )(rows, block_ids, ranks, w_in, w_hid, w_out, w_dens)


def with_halo(shard, sides, width):
    for axis, dim in sides:
        peers, length = (lax.axis_size(axis), shard.shape[dim])
        up = [(i, (i + 1) % peers) for i in range(peers - 1)]
        down = [(j, i) for i, j in up]
        last = lax.slice_in_dim(shard, length - width, length, axis=dim)
        initial = lax.slice_in_dim(shard, 0, width, axis=dim)
        before = lax.ppermute(last, axis, up)
        after = lax.ppermute(initial, axis, down)
        shard = jnp.concatenate([before, shard, after], axis=dim)
    return shard


def conv_layer(padded, kernel, out_rows, out_cols):
    pieces = []
    for offset_y in range(3):
        for offset_x in range(3):
            pieces.append(padded[offset_y : offset_y + out_rows, offset_x : offset_x + out_cols])
    patches = jnp.concatenate(pieces, axis=-1)
    channels = kernel.shape[-1]
    result = jnp.dot(
        patches, kernel.reshape(9 * kernel.shape[2], channels), preferred_element_type=jnp.float32
    )
    center = padded[1 : 1 + out_rows, 1 : 1 + out_cols].astype(jnp.float32)
    return (center + jax.nn.silu(result)).astype(jnp.bfloat16)


def shards(seg_feat, seg_block, depth_rank, w_in, w_hidden, w_out, w_dens, conv_w):
    block_count = lax.axis_size("blocks")
    segments = seg_feat.shape[2]
    color = render(
        block_count,
        seg_feat[0, 0],
        seg_block.reshape(1, segments),
        depth_rank[0, 0],
        w_in[0],
        w_hidden[0],
        w_out[0],
        w_dens,
    )
    tile_image = color.reshape(TH, TW, color.shape[1])
    rows_total = TH * lax.axis_size(("tiles", "sub"))
    cols_total = TW * block_count
    row_pos = (
        lax.axis_index(("tiles", "sub")) * TH
        - CONV_LAYERS
        + jnp.arange(TH + 2 * CONV_LAYERS, dtype=jnp.int32)
    )
    col_pos = (
        lax.axis_index("blocks") * TW
        - CONV_LAYERS
        + jnp.arange(TW + 2 * CONV_LAYERS, dtype=jnp.int32)
    )
    inside = ((row_pos >= 0) & (row_pos < rows_total))[:, None] & (
        (col_pos >= 0) & (col_pos < cols_total)
    )[None, :]
    current = with_halo(tile_image, (("blocks", 1), (("tiles", "sub"), 0)), CONV_LAYERS)
    for layer_index in range(CONV_LAYERS):
        margin = CONV_LAYERS - layer_index - 1
        size_h = TH + 2 * margin
        size_w = TW + 2 * margin
        current = conv_layer(current, conv_w[layer_index], size_h, size_w)
        keep_mask = inside[
            layer_index + 1 : layer_index + 1 + size_h, layer_index + 1 : layer_index + 1 + size_w
        ]
        current = jnp.where(keep_mask[:, :, None], current, jnp.zeros_like(current))
    tile_image = current
    return tile_image


def solution(mesh):
    in_specs = (
        P(("groups", "tiles", "sub"), "blocks", None, None),
        P(("groups", "tiles", "sub"), "blocks", None, None),
        P(("groups", "tiles", "sub"), "blocks", None, None),
        P("blocks", None, None),
        P("blocks", None, None, None),
        P("blocks", None, None),
        P("blocks", None),
        P(),
    )
    out_specs = P(("groups", "tiles", "sub"), "blocks", None)
    return jax.shard_map(shards, mesh=mesh, in_specs=in_specs, out_specs=out_specs, check_vma=False)
```

```python
import functools

import jax
import jax.numpy as jnp
from jax import lax
from jax.experimental import pallas as pl
from jax.experimental.pallas import tpu as pltpu
from jax.sharding import PartitionSpec as P

SEGS_RAY = 8
CONV_LAYERS = 3
TW = 16
TH = 16
RAYS_DEV = 256
MESH = pl.DeviceIdType.MESH
F32 = jnp.float32
BF16 = jnp.bfloat16


def silu(value):
    half = 0.5 * value
    return half + half * jnp.tanh(half)


def softplus(value):
    return jnp.maximum(value, 0.0) + jnp.log1p(jnp.exp(-jnp.abs(value)))


def block_at(step, place, count):
    near = jnp.minimum(place, count - 1 - place)
    distance = (step + 1) // 2
    paired = jnp.where(step % 2 == 1, place + distance, place - distance)
    rest = jnp.where(2 * place <= count - 1, step, count - 1 - step)
    return jnp.where(step <= 2 * near, paired, rest)


Z, X, Y, D, SA, SX, SY, SD, ZD = range(9)


def render_kernel(
    count,
    capacity,
    row_tile,
    feat_ref,
    block_ref,
    rank_ref,
    w_in_ref,
    w_hid_ref,
    w_out_ref,
    w_dens_ref,
    color_ref,
    hid,
    ends,
    slot_row,
    wide,
    turns,
    rays,
    act,
    heads,
    dens_map,
    send_sem,
    recv_sem,
    ends_send,
    ends_recv,
    own_sem,
):
    place = lax.axis_index("blocks")
    tile = lax.axis_index("tiles")
    group = lax.axis_index("groups")
    core = lax.axis_index("sub")
    tile_mate = tile + 1 - 2 * (tile % 2)
    group_mate = group + 1 - 2 * (group % 2)
    core_mate = 1 - core
    tx, gy = tile % 2, group % 2
    layers = w_hid_ref.shape[0]
    hidden = w_hid_ref.shape[2]
    part = hidden // 8
    end_rows = ends.shape[1]
    end_half = end_rows // 2
    feats = w_out_ref.shape[1]
    in_width = w_in_ref.shape[0]
    segments = feat_ref.shape[0]

    def eighth(a, b, c):
        return (a * 2 + b) * 2 + c

    to_x, to_y, to_c = {"tiles": tile_mate}, {"groups": group_mate}, {"sub": core_mate}

    barrier = pltpu.get_barrier_semaphore()
    pl.semaphore_signal(barrier, inc=1, device_id=to_x, device_id_type=MESH)
    pl.semaphore_signal(barrier, inc=1, device_id=to_y, device_id_type=MESH)
    pl.semaphore_signal(barrier, inc=1, device_id=to_c, device_id_type=MESH)

    @pl.when(place > 0)
    def _():
        pl.semaphore_signal(barrier, inc=1, device_id={"blocks": place - 1}, device_id_type=MESH)

    @pl.when(place < count - 1)
    def _():
        pl.semaphore_signal(barrier, inc=1, device_id={"blocks": place + 1}, device_id_type=MESH)

    own = pltpu.make_async_copy(w_hid_ref, hid.at[place], own_sem)
    own.start()
    ends[place, 0:in_width] = w_in_ref[...]
    ends[place, in_width : in_width + feats] = w_out_ref[...].T
    ends[place, in_width + feats : end_rows] = jnp.broadcast_to(
        w_dens_ref[...], (end_rows - in_width - feats, hidden)
    )
    own.wait()

    peers = 3 + jnp.minimum(place, 1) + jnp.minimum(count - 1 - place, 1)
    pl.semaphore_wait(barrier, peers)

    def piece(block, layer, which):
        return hid.at[block, layer, pl.ds(pl.multiple_of(which * part, part), part)]

    def move(block, layer, which, kind, target, send_kind=None):
        ref = piece(block, layer, which)
        return pltpu.make_async_remote_copy(
            src_ref=ref,
            dst_ref=ref,
            send_sem=send_sem.at[block, layer, kind if send_kind is None else send_kind],
            recv_sem=recv_sem.at[block, layer, kind],
            device_id=target,
            device_id_type=MESH,
        )

    def move_ends(block, half, kind, target, send_kind=None):
        ref = ends.at[block, pl.ds(pl.multiple_of(half * end_half, end_half), end_half)]
        return pltpu.make_async_remote_copy(
            src_ref=ref,
            dst_ref=ref,
            send_sem=ends_send.at[block, kind if send_kind is None else send_kind],
            recv_sem=ends_recv.at[block, kind],
            device_id=target,
            device_id_type=MESH,
        )

    e_own = eighth(tx, gy, core)
    e_x = eighth(1 - tx, gy, core)
    e_y = eighth(tx, 1 - gy, core)
    e_d = eighth(1 - tx, 1 - gy, core)
    m_own = eighth(tx, gy, core_mate)
    m_x = eighth(1 - tx, gy, core_mate)
    m_y = eighth(tx, 1 - gy, core_mate)
    m_d = eighth(1 - tx, 1 - gy, core_mate)
    up, down = {"blocks": place + 1}, {"blocks": place - 1}

    def own_up(action):
        @pl.when(place < count - 1)
        def _():
            action(move_ends(place, core, 0, up))
            for layer in range(layers):
                action(move(place, layer, e_own, Z, up))

    def own_down(action):
        @pl.when(place > 0)
        def _():
            action(move_ends(place, core, 0, down, 2))
            for layer in range(layers):
                action(move(place, layer, e_own, Z, down, ZD))

    own_up(lambda c: c.start())
    own_down(lambda c: c.start())

    def onward(block, action):
        @pl.when((block < place) & (place < count - 1))
        def _():
            action(up)

        @pl.when((block > place) & (place > 0))
        def _():
            action(down)

    def arrive(block, layer):
        move(block, layer, e_own, Z, up).wait_recv()
        onward(block, lambda to: move(block, layer, e_own, Z, to).start())
        move(block, layer, e_own, X, to_x).start()
        move(block, layer, e_own, Y, to_y).start()
        move(block, layer, e_own, SA, to_c).start()

    def arrive_ends(block):
        move_ends(block, core, 0, up).wait_recv()
        onward(block, lambda to: move_ends(block, core, 0, to).start())
        move_ends(block, core, 1, to_c).start()

    def cross(block, layer):
        move(block, layer, e_x, X, to_x).wait_recv()
        move(block, layer, e_y, Y, to_y).wait_recv()

        @pl.when(core == 0)
        def _():
            move(block, layer, e_x, D, to_y).start()

        @pl.when(core == 1)
        def _():
            move(block, layer, e_y, D, to_x).start()

        move(block, layer, e_x, SX, to_c).start()
        move(block, layer, e_y, SY, to_c).start()

    def corner(block, layer):
        move(block, layer, e_d, D, to_x).wait_recv()
        move(block, layer, e_d, SD, to_c).start()

    def ready(block, layer):
        move(block, layer, m_own, SA, to_c).wait_recv()
        move(block, layer, m_x, SX, to_c).wait_recv()
        move(block, layer, m_y, SY, to_c).wait_recv()
        move(block, layer, m_d, SD, to_c).wait_recv()

    def item(step, layer, ahead):
        return step + (layer + ahead) // layers, (layer + ahead) % layers

    def exchange(step, layer):
        for ahead, action in ((4, arrive), (3, cross), (2, corner)):
            later, its_layer = item(step, layer, ahead)

            @pl.when((later > 0) & (later < count))
            def _():
                block = block_at(later, place, count)
                if action is arrive and its_layer == 0:
                    arrive_ends(block)
                action(block, its_layer)

    rows16 = 16
    lane = lax.broadcasted_iota(jnp.int32, (128, 128), 1)
    sub = lax.broadcasted_iota(jnp.int32, (128, 128), 0)
    earlier = (sub < lane).astype(F32).astype(BF16)
    names = lax.broadcasted_iota(jnp.int32, (rows16, 128), 0)
    base = names.astype(F32) * capacity
    carry = jnp.zeros((rows16, 1), F32)
    for chunk in range(segments // 128):
        cols = slice(chunk * 128, (chunk + 1) * 128)
        named = (jnp.broadcast_to(block_ref[:, cols], (rows16, 128)) == names).astype(F32)
        before = jnp.dot(named.astype(BF16), earlier, preferred_element_type=F32) + carry
        carry = carry + jnp.sum(named, axis=1, keepdims=True)
        slots = jnp.sum(named * (before + base), axis=0, keepdims=True)
        slot_row[:, cols] = slots.astype(jnp.int32)
    wide[:, 0:in_width] = feat_ref[...]
    row_of = lax.broadcasted_iota(jnp.int32, (segments, 128), 0)
    lane_of = lax.broadcasted_iota(jnp.int32, (segments, 128), 1)
    ray, turn = row_of % RAYS_DEV, row_of // RAYS_DEV
    tags = jnp.where(lane_of == SEGS_RAY, ray, jnp.where(lane_of == turn, 1, 0))
    wide[:, in_width : in_width + 128] = tags.astype(F32).astype(BF16)
    dens_map[...] = jnp.zeros_like(dens_map)

    tiles_n = capacity // row_tile

    def tile_loop(body):
        for index in range(tiles_n):
            body(slice(index * row_tile, (index + 1) * row_tile), index)

    rows_first = (((0,), (0,)), ((), ()))

    def gather_in(step, block):
        def body(rows, index):
            wanted = (
                lax.broadcasted_iota(jnp.int32, (row_tile, segments), 0)
                + block * capacity
                + index * row_tile
            )
            pick = (slot_row[...] == wanted).astype(F32).astype(BF16)
            mine = jnp.dot(pick, wide[...], preferred_element_type=F32)
            tag = mine[:, in_width : in_width + 128]
            turns[step, rows] = jnp.where(lane_tile < SEGS_RAY, tag, 0.0).astype(BF16)
            on_ray = lax.broadcasted_iota(jnp.int32, (row_tile, RAYS_DEV), 1).astype(F32)
            rays[step, rows] = (tag[:, SEGS_RAY : SEGS_RAY + 1] == on_ray).astype(F32).astype(BF16)
            act[rows] = silu(
                jnp.dot(
                    mine[:, 0:in_width].astype(BF16),
                    ends[block, 0:in_width],
                    preferred_element_type=F32,
                )
            ).astype(BF16)

        tile_loop(body)

    lane_tile = lax.broadcasted_iota(jnp.int32, (row_tile, 128), 1)

    def layer_step(block, layer):
        def body(rows, index):
            value = act[rows]
            update = silu(jnp.dot(value, hid[block, layer], preferred_element_type=F32))
            act[rows] = (value.astype(F32) + update).astype(BF16)

        tile_loop(body)

    def head_step(step, block):
        w_den = jnp.broadcast_to(ends[block, in_width + feats : in_width + feats + 1], (128, hidden))
        w_head = jnp.concatenate([ends[block, in_width : in_width + feats], w_den], axis=0)
        contract = (((1,), (1,)), ((), ()))

        def body(rows, index):
            out = lax.dot_general(act[rows], w_head, contract, preferred_element_type=F32)
            heads[step, rows] = out[:, 0:feats].astype(BF16)
            density = (0.25 * softplus(out[:, feats : feats + 128])).astype(BF16)
            dens_map[...] += lax.dot_general(
                turns[step, rows] * density, rays[step, rows], rows_first, preferred_element_type=F32
            )

        tile_loop(body)

    def step_body(step, carry_in):
        block = block_at(step, place, count)
        for layer in range(layers):
            exchange(step, layer)

            @pl.when(step > 0)
            def _():
                if layer == 0:
                    move_ends(block, core_mate, 1, to_c).wait_recv()
                ready(block, layer)

            if layer == 0:
                gather_in(step, block)
            layer_step(block, layer)
        head_step(step, block)
        return carry_in

    lax.fori_loop(0, count, step_body, 0)

    density = dens_map[0:SEGS_RAY]
    optical = jnp.zeros((SEGS_RAY, RAYS_DEV), F32)
    for k in range(SEGS_RAY):
        nearer = rank_ref[k : k + 1, :] < rank_ref[...]
        optical += jnp.where(nearer, density[k : k + 1], 0.0)
    weight = jnp.exp(-optical) * (1.0 - jnp.exp(-density))
    weight = jnp.concatenate([weight, jnp.zeros((128 - SEGS_RAY, RAYS_DEV), F32)], axis=0)
    coarse = weight.astype(BF16)
    fine = (weight - coarse.astype(F32)).astype(BF16)

    def blend(step, color):
        turn_rows, ray_rows, head_rows = turns[step], rays[step], heads[step]
        for share in (coarse, fine):
            spread = jnp.dot(turn_rows, share, preferred_element_type=F32).astype(BF16) * ray_rows
            color += lax.dot_general(
                head_rows, spread, rows_first, preferred_element_type=F32
            )
        return color

    color = lax.fori_loop(0, count, blend, jnp.zeros((feats, RAYS_DEV), F32))
    color_ref[...] = color.T.astype(BF16)

    own_up(lambda c: c.wait_send())
    own_down(lambda c: c.wait_send())

    def drain(step, carry_in):
        block = block_at(step, place, count)
        onward(block, lambda to: move_ends(block, core, 0, to).wait_send())
        move_ends(block, core, 1, to_c).wait_send()
        for layer in range(layers):
            onward(block, lambda to, layer=layer: move(block, layer, e_own, Z, to).wait_send())
            for kind in (X, Y, D, SA, SX, SY, SD):
                move(block, layer, e_own, kind, to_c).wait_send()
        return carry_in

    lax.fori_loop(1, count, drain, 0)


def render(count, rows, block_ids, ranks, w_in, w_hid, w_out, w_dens):
    segments, in_width = rows.shape
    capacity = 2 * segments // count
    layers, hidden, _ = w_hid.shape
    feats = w_out.shape[1]
    row_tile = min(512, capacity)
    end_rows = in_width + feats + 32
    vmem = pl.BlockSpec(memory_space=pltpu.VMEM)
    macs = count * capacity * hidden * (in_width + layers * hidden + feats)
    return pl.pallas_call(
        functools.partial(render_kernel, count, capacity, row_tile),
        out_shape=jax.ShapeDtypeStruct((RAYS_DEV, feats), BF16),
        in_specs=[vmem, vmem, vmem, vmem, pl.BlockSpec(memory_space=pl.ANY), vmem, vmem],
        out_specs=vmem,
        scratch_shapes=[
            pltpu.VMEM((count, layers, hidden, hidden), BF16),
            pltpu.VMEM((count, end_rows, hidden), BF16),
            pltpu.VMEM((1, segments), jnp.int32),
            pltpu.VMEM((segments, in_width + 128), BF16),
            pltpu.VMEM((count, capacity, 128), BF16),
            pltpu.VMEM((count, capacity, RAYS_DEV), BF16),
            pltpu.VMEM((capacity, hidden), BF16),
            pltpu.VMEM((count, capacity, feats), BF16),
            pltpu.VMEM((128, RAYS_DEV), F32),
            pltpu.SemaphoreType.DMA((count, layers, 9)),
            pltpu.SemaphoreType.DMA((count, layers, 8)),
            pltpu.SemaphoreType.DMA((count, 3)),
            pltpu.SemaphoreType.DMA((count, 2)),
            pltpu.SemaphoreType.DMA,
        ],
        compiler_params=pltpu.CompilerParams(
            collective_id=0, has_side_effects=True, vmem_limit_bytes=56 * 1024 * 1024
        ),
        cost_estimate=pl.CostEstimate(flops=2 * macs, bytes_accessed=4 << 20, transcendentals=0),
        name="render",
    )(rows, block_ids, ranks, w_in, w_hid, w_out, w_dens)


def with_halo(shard, sides, width):
    for axis, dim in sides:
        peers, length = (lax.axis_size(axis), shard.shape[dim])
        up = [(i, (i + 1) % peers) for i in range(peers - 1)]
        down = [(j, i) for i, j in up]
        last = lax.slice_in_dim(shard, length - width, length, axis=dim)
        initial = lax.slice_in_dim(shard, 0, width, axis=dim)
        before = lax.ppermute(last, axis, up)
        after = lax.ppermute(initial, axis, down)
        shard = jnp.concatenate([before, shard, after], axis=dim)
    return shard


def conv_layer(padded, kernel, out_rows, out_cols):
    pieces = []
    for offset_y in range(3):
        for offset_x in range(3):
            pieces.append(padded[offset_y : offset_y + out_rows, offset_x : offset_x + out_cols])
    patches = jnp.concatenate(pieces, axis=-1)
    channels = kernel.shape[-1]
    result = jnp.dot(
        patches, kernel.reshape(9 * kernel.shape[2], channels), preferred_element_type=jnp.float32
    )
    center = padded[1 : 1 + out_rows, 1 : 1 + out_cols].astype(jnp.float32)
    return (center + jax.nn.silu(result)).astype(jnp.bfloat16)


def shards(seg_feat, seg_block, depth_rank, w_in, w_hidden, w_out, w_dens, conv_w):
    block_count = lax.axis_size("blocks")
    segments = seg_feat.shape[2]
    color = render(
        block_count,
        seg_feat[0, 0],
        seg_block.reshape(1, segments),
        depth_rank[0, 0],
        w_in[0],
        w_hidden[0],
        w_out[0],
        w_dens,
    )
    tile_image = color.reshape(TH, TW, color.shape[1])
    rows_total = TH * lax.axis_size(("tiles", "sub"))
    cols_total = TW * block_count
    row_pos = (
        lax.axis_index(("tiles", "sub")) * TH
        - CONV_LAYERS
        + jnp.arange(TH + 2 * CONV_LAYERS, dtype=jnp.int32)
    )
    col_pos = (
        lax.axis_index("blocks") * TW
        - CONV_LAYERS
        + jnp.arange(TW + 2 * CONV_LAYERS, dtype=jnp.int32)
    )
    inside = ((row_pos >= 0) & (row_pos < rows_total))[:, None] & (
        (col_pos >= 0) & (col_pos < cols_total)
    )[None, :]
    current = with_halo(tile_image, (("blocks", 1), (("tiles", "sub"), 0)), CONV_LAYERS)
    for layer_index in range(CONV_LAYERS):
        margin = CONV_LAYERS - layer_index - 1
        size_h = TH + 2 * margin
        size_w = TW + 2 * margin
        current = conv_layer(current, conv_w[layer_index], size_h, size_w)
        keep_mask = inside[
            layer_index + 1 : layer_index + 1 + size_h, layer_index + 1 : layer_index + 1 + size_w
        ]
        current = jnp.where(keep_mask[:, :, None], current, jnp.zeros_like(current))
    tile_image = current
    return tile_image


def solution(mesh):
    in_specs = (
        P(("groups", "tiles", "sub"), "blocks", None, None),
        P(("groups", "tiles", "sub"), "blocks", None, None),
        P(("groups", "tiles", "sub"), "blocks", None, None),
        P("blocks", None, None),
        P("blocks", None, None, None),
        P("blocks", None, None),
        P("blocks", None),
        P(),
    )
    out_specs = P(("groups", "tiles", "sub"), "blocks", None)
    return jax.shard_map(shards, mesh=mesh, in_specs=in_specs, out_specs=out_specs, check_vma=False)
```

```python
import functools

import jax
import jax.numpy as jnp
from jax import lax
from jax.experimental import pallas as pl
from jax.experimental.pallas import tpu as pltpu
from jax.sharding import PartitionSpec as P

SEGS_RAY = 8
CONV_LAYERS = 3
TW = 16
TH = 16
RAYS_DEV = 256
MESH = pl.DeviceIdType.MESH
F32 = jnp.float32
BF16 = jnp.bfloat16


def silu(value):
    half = value * jnp.asarray(0.5, value.dtype)
    return half + half * jnp.tanh(half)


def softplus(value):
    return jnp.maximum(value, 0.0) + jnp.log1p(jnp.exp(-jnp.abs(value)))


def block_at(step, place, count):
    near = jnp.minimum(place, count - 1 - place)
    distance = (step + 1) // 2
    paired = jnp.where(step % 2 == 1, place + distance, place - distance)
    rest = jnp.where(2 * place <= count - 1, step, count - 1 - step)
    return jnp.where(step <= 2 * near, paired, rest)


Z, X, Y, D, SA, SX, SY, SD, ZD = range(9)


def render_kernel(
    count,
    capacity,
    row_tile,
    feat_ref,
    block_ref,
    rank_ref,
    w_in_ref,
    w_hid_ref,
    w_out_ref,
    w_dens_ref,
    color_ref,
    hid,
    ends,
    slot_row,
    wide,
    turns,
    rays,
    act,
    heads,
    dens_map,
    send_sem,
    recv_sem,
    ends_send,
    ends_recv,
    own_sem,
):
    place = lax.axis_index("blocks")
    tile = lax.axis_index("tiles")
    group = lax.axis_index("groups")
    core = lax.axis_index("sub")
    tile_mate = tile + 1 - 2 * (tile % 2)
    group_mate = group + 1 - 2 * (group % 2)
    core_mate = 1 - core
    tx, gy = tile % 2, group % 2
    layers = w_hid_ref.shape[0]
    hidden = w_hid_ref.shape[2]
    part = hidden // 8
    end_rows = ends.shape[1]
    end_half = end_rows // 2
    feats = w_out_ref.shape[1]
    in_width = w_in_ref.shape[0]
    segments = feat_ref.shape[0]

    def eighth(a, b, c):
        return (a * 2 + b) * 2 + c

    to_x, to_y, to_c = {"tiles": tile_mate}, {"groups": group_mate}, {"sub": core_mate}

    barrier = pltpu.get_barrier_semaphore()
    pl.semaphore_signal(barrier, inc=1, device_id=to_x, device_id_type=MESH)
    pl.semaphore_signal(barrier, inc=1, device_id=to_y, device_id_type=MESH)
    pl.semaphore_signal(barrier, inc=1, device_id=to_c, device_id_type=MESH)

    @pl.when(place > 0)
    def _():
        pl.semaphore_signal(barrier, inc=1, device_id={"blocks": place - 1}, device_id_type=MESH)

    @pl.when(place < count - 1)
    def _():
        pl.semaphore_signal(barrier, inc=1, device_id={"blocks": place + 1}, device_id_type=MESH)

    own = pltpu.make_async_copy(w_hid_ref, hid.at[place], own_sem)
    own.start()
    ends[place, 0:in_width] = w_in_ref[...]
    ends[place, in_width : in_width + feats] = w_out_ref[...].T
    ends[place, in_width + feats : end_rows] = jnp.broadcast_to(
        w_dens_ref[...], (end_rows - in_width - feats, hidden)
    )
    own.wait()

    peers = 3 + jnp.minimum(place, 1) + jnp.minimum(count - 1 - place, 1)
    pl.semaphore_wait(barrier, peers)

    def piece(block, layer, which):
        return hid.at[block, layer, pl.ds(pl.multiple_of(which * part, part), part)]

    def move(block, layer, which, kind, target, send_kind=None):
        ref = piece(block, layer, which)
        return pltpu.make_async_remote_copy(
            src_ref=ref,
            dst_ref=ref,
            send_sem=send_sem.at[block, layer, kind if send_kind is None else send_kind],
            recv_sem=recv_sem.at[block, layer, kind],
            device_id=target,
            device_id_type=MESH,
        )

    def move_ends(block, half, kind, target, send_kind=None):
        ref = ends.at[block, pl.ds(pl.multiple_of(half * end_half, end_half), end_half)]
        return pltpu.make_async_remote_copy(
            src_ref=ref,
            dst_ref=ref,
            send_sem=ends_send.at[block, kind if send_kind is None else send_kind],
            recv_sem=ends_recv.at[block, kind],
            device_id=target,
            device_id_type=MESH,
        )

    e_own = eighth(tx, gy, core)
    e_x = eighth(1 - tx, gy, core)
    e_y = eighth(tx, 1 - gy, core)
    e_d = eighth(1 - tx, 1 - gy, core)
    m_own = eighth(tx, gy, core_mate)
    m_x = eighth(1 - tx, gy, core_mate)
    m_y = eighth(tx, 1 - gy, core_mate)
    m_d = eighth(1 - tx, 1 - gy, core_mate)
    up, down = {"blocks": place + 1}, {"blocks": place - 1}

    def own_up(action):
        @pl.when(place < count - 1)
        def _():
            action(move_ends(place, core, 0, up))
            for layer in range(layers):
                action(move(place, layer, e_own, Z, up))

    def own_down(action):
        @pl.when(place > 0)
        def _():
            action(move_ends(place, core, 0, down, 2))
            for layer in range(layers):
                action(move(place, layer, e_own, Z, down, ZD))

    own_up(lambda c: c.start())
    own_down(lambda c: c.start())

    def onward(block, action):
        @pl.when((block < place) & (place < count - 1))
        def _():
            action(up)

        @pl.when((block > place) & (place > 0))
        def _():
            action(down)

    def arrive(block, layer):
        move(block, layer, e_own, Z, up).wait_recv()
        onward(block, lambda to: move(block, layer, e_own, Z, to).start())
        move(block, layer, e_own, X, to_x).start()
        move(block, layer, e_own, Y, to_y).start()
        move(block, layer, e_own, SA, to_c).start()

    def arrive_ends(block):
        move_ends(block, core, 0, up).wait_recv()
        onward(block, lambda to: move_ends(block, core, 0, to).start())
        move_ends(block, core, 1, to_c).start()

    def cross(block, layer):
        move(block, layer, e_x, X, to_x).wait_recv()
        move(block, layer, e_y, Y, to_y).wait_recv()

        @pl.when(core == 0)
        def _():
            move(block, layer, e_x, D, to_y).start()

        @pl.when(core == 1)
        def _():
            move(block, layer, e_y, D, to_x).start()

        move(block, layer, e_x, SX, to_c).start()
        move(block, layer, e_y, SY, to_c).start()

    def corner(block, layer):
        move(block, layer, e_d, D, to_x).wait_recv()
        move(block, layer, e_d, SD, to_c).start()

    def ready(block, layer):
        move(block, layer, m_own, SA, to_c).wait_recv()
        move(block, layer, m_x, SX, to_c).wait_recv()
        move(block, layer, m_y, SY, to_c).wait_recv()
        move(block, layer, m_d, SD, to_c).wait_recv()

    def item(step, layer, ahead):
        return step + (layer + ahead) // layers, (layer + ahead) % layers

    def exchange(step, layer):
        for ahead, action in ((4, arrive), (3, cross), (2, corner)):
            later, its_layer = item(step, layer, ahead)

            @pl.when((later > 0) & (later < count))
            def _():
                block = block_at(later, place, count)
                if action is arrive and its_layer == 0:
                    arrive_ends(block)
                action(block, its_layer)

    rows16 = 16
    chunks = segments // 128
    lane = lax.broadcasted_iota(jnp.int32, (128, 128), 1)
    sub = lax.broadcasted_iota(jnp.int32, (128, 128), 0)
    earlier = (sub < lane).astype(F32).astype(BF16)
    names = lax.broadcasted_iota(jnp.int32, (rows16, 128), 0)
    base = names.astype(F32) * capacity
    named = [
        (jnp.broadcast_to(block_ref[:, c * 128 : (c + 1) * 128], (rows16, 128)) == names).astype(F32)
        for c in range(chunks)
    ]
    before = jnp.dot(
        jnp.concatenate(named, axis=0).astype(BF16), earlier, preferred_element_type=F32
    )
    carry = base
    for c in range(chunks):
        ahead_of = before[c * rows16 : (c + 1) * rows16] + carry
        carry = carry + jnp.sum(named[c], axis=1, keepdims=True)
        slot_row[:, c * 128 : (c + 1) * 128] = jnp.sum(named[c] * ahead_of, axis=0, keepdims=True)
    wide[:, 0:in_width] = feat_ref[...]
    ray_of = lax.broadcasted_iota(jnp.int32, (RAYS_DEV, 128), 0)
    lane_of = lax.broadcasted_iota(jnp.int32, (RAYS_DEV, 128), 1)
    ray_tag = jnp.where(lane_of == SEGS_RAY, ray_of, 0)
    for k in range(SEGS_RAY):
        tags = jnp.where(lane_of == k, 1, ray_tag)
        wide[k * RAYS_DEV : (k + 1) * RAYS_DEV, in_width : in_width + 128] = tags.astype(F32).astype(
            BF16
        )
    dens_map[...] = jnp.zeros_like(dens_map)

    pick_tile = min(256, capacity)

    def tile_loop(body, size):
        for index in range(capacity // size):
            body(slice(index * size, (index + 1) * size), index)

    rows_first = (((0,), (0,)), ((), ()))

    def gather_in(step, block):
        def body(rows, index):
            first = (block * capacity + index * pick_tile).astype(F32)
            held = jnp.clip(slot_row[...] - first, -1.0, float(pick_tile)).astype(BF16)
            wanted = lax.broadcasted_iota(jnp.int32, (pick_tile, segments), 0).astype(F32).astype(BF16)
            same = jnp.broadcast_to(held, (pick_tile, segments)) == wanted
            pick = jnp.where(same, jnp.ones((), BF16), jnp.zeros((), BF16))
            mine = jnp.dot(pick, wide[...], preferred_element_type=F32)
            tag = mine[:, in_width : in_width + 128]
            turns[step, rows] = jnp.where(lane_tile < SEGS_RAY, tag, 0.0).astype(BF16)
            on_ray = lax.broadcasted_iota(jnp.int32, (pick_tile, RAYS_DEV), 1).astype(F32)
            rays[step, rows] = (tag[:, SEGS_RAY : SEGS_RAY + 1] == on_ray).astype(F32).astype(BF16)
            act[rows] = silu(
                jnp.dot(
                    mine[:, 0:in_width].astype(BF16),
                    ends[block, 0:in_width],
                    preferred_element_type=F32,
                ).astype(BF16)
            )

        tile_loop(body, pick_tile)

    lane_tile = lax.broadcasted_iota(jnp.int32, (pick_tile, 128), 1)

    def layer_step(block, layer):
        def body(rows, index):
            value = act[rows]
            act[rows] = value + silu(
                jnp.dot(value, hid[block, layer], preferred_element_type=F32).astype(BF16)
            )

        tile_loop(body, row_tile)

    def head_step(step, block):
        w_den = jnp.broadcast_to(ends[block, in_width + feats : in_width + feats + 1], (128, hidden))
        w_head = jnp.concatenate([ends[block, in_width : in_width + feats], w_den], axis=0)
        contract = (((1,), (1,)), ((), ()))

        def body(rows, index):
            out = lax.dot_general(act[rows], w_head, contract, preferred_element_type=F32)
            heads[step, rows] = out[:, 0:feats].astype(BF16)
            density = (0.25 * softplus(out[:, feats : feats + 128])).astype(BF16)
            dens_map[...] += lax.dot_general(
                turns[step, rows] * density, rays[step, rows], rows_first, preferred_element_type=F32
            )

        tile_loop(body, row_tile)

    def step_body(step, carry_in):
        block = block_at(step, place, count)
        for layer in range(layers):
            exchange(step, layer)

            @pl.when(step > 0)
            def _():
                if layer == 0:
                    move_ends(block, core_mate, 1, to_c).wait_recv()
                ready(block, layer)

            if layer == 0:
                gather_in(step, block)
            layer_step(block, layer)
        head_step(step, block)
        return carry_in

    lax.fori_loop(0, count, step_body, 0)

    density = dens_map[0:SEGS_RAY]
    optical = jnp.zeros((SEGS_RAY, RAYS_DEV), F32)
    for k in range(SEGS_RAY):
        nearer = rank_ref[k : k + 1, :] < rank_ref[...]
        optical += jnp.where(nearer, density[k : k + 1], 0.0)
    weight = jnp.exp(-optical) * (1.0 - jnp.exp(-density))
    weight = jnp.concatenate([weight, jnp.zeros((128 - SEGS_RAY, RAYS_DEV), F32)], axis=0)
    weight = weight.astype(BF16)

    def blend(step, color):
        spread = jnp.dot(turns[step], weight, preferred_element_type=F32).astype(BF16) * rays[step]
        return color + lax.dot_general(heads[step], spread, rows_first, preferred_element_type=F32)

    color = lax.fori_loop(0, count, blend, jnp.zeros((feats, RAYS_DEV), F32))
    color_ref[...] = color.T.astype(BF16)

    own_up(lambda c: c.wait_send())
    own_down(lambda c: c.wait_send())

    def drain(step, carry_in):
        block = block_at(step, place, count)
        onward(block, lambda to: move_ends(block, core, 0, to).wait_send())
        move_ends(block, core, 1, to_c).wait_send()
        for layer in range(layers):
            onward(block, lambda to, layer=layer: move(block, layer, e_own, Z, to).wait_send())
            for kind in (X, Y, D, SA, SX, SY, SD):
                move(block, layer, e_own, kind, to_c).wait_send()
        return carry_in

    lax.fori_loop(1, count, drain, 0)


def render(count, rows, block_ids, ranks, w_in, w_hid, w_out, w_dens):
    segments, in_width = rows.shape
    capacity = 2 * segments // count
    layers, hidden, _ = w_hid.shape
    feats = w_out.shape[1]
    row_tile = min(512, capacity)
    end_rows = in_width + feats + 32
    vmem = pl.BlockSpec(memory_space=pltpu.VMEM)
    macs = count * capacity * hidden * (in_width + layers * hidden + feats)
    return pl.pallas_call(
        functools.partial(render_kernel, count, capacity, row_tile),
        out_shape=jax.ShapeDtypeStruct((RAYS_DEV, feats), BF16),
        in_specs=[vmem, vmem, vmem, vmem, pl.BlockSpec(memory_space=pl.ANY), vmem, vmem],
        out_specs=vmem,
        scratch_shapes=[
            pltpu.VMEM((count, layers, hidden, hidden), BF16),
            pltpu.VMEM((count, end_rows, hidden), BF16),
            pltpu.VMEM((1, segments), F32),
            pltpu.VMEM((segments, in_width + 128), BF16),
            pltpu.VMEM((count, capacity, 128), BF16),
            pltpu.VMEM((count, capacity, RAYS_DEV), BF16),
            pltpu.VMEM((capacity, hidden), BF16),
            pltpu.VMEM((count, capacity, feats), BF16),
            pltpu.VMEM((128, RAYS_DEV), F32),
            pltpu.SemaphoreType.DMA((count, layers, 9)),
            pltpu.SemaphoreType.DMA((count, layers, 8)),
            pltpu.SemaphoreType.DMA((count, 3)),
            pltpu.SemaphoreType.DMA((count, 2)),
            pltpu.SemaphoreType.DMA,
        ],
        compiler_params=pltpu.CompilerParams(
            collective_id=0, has_side_effects=True, vmem_limit_bytes=56 * 1024 * 1024
        ),
        cost_estimate=pl.CostEstimate(flops=2 * macs, bytes_accessed=4 << 20, transcendentals=0),
        name="render",
    )(rows, block_ids, ranks, w_in, w_hid, w_out, w_dens)


def with_halo(shard, sides, width):
    for axis, dim in sides:
        peers, length = (lax.axis_size(axis), shard.shape[dim])
        up = [(i, (i + 1) % peers) for i in range(peers - 1)]
        down = [(j, i) for i, j in up]
        last = lax.slice_in_dim(shard, length - width, length, axis=dim)
        initial = lax.slice_in_dim(shard, 0, width, axis=dim)
        before = lax.ppermute(last, axis, up)
        after = lax.ppermute(initial, axis, down)
        shard = jnp.concatenate([before, shard, after], axis=dim)
    return shard


def conv_layer(padded, kernel, out_rows, out_cols):
    pieces = []
    for offset_y in range(3):
        for offset_x in range(3):
            pieces.append(padded[offset_y : offset_y + out_rows, offset_x : offset_x + out_cols])
    patches = jnp.concatenate(pieces, axis=-1)
    channels = kernel.shape[-1]
    result = jnp.dot(
        patches, kernel.reshape(9 * kernel.shape[2], channels), preferred_element_type=jnp.float32
    )
    center = padded[1 : 1 + out_rows, 1 : 1 + out_cols].astype(jnp.float32)
    return (center + jax.nn.silu(result)).astype(jnp.bfloat16)


def shards(seg_feat, seg_block, depth_rank, w_in, w_hidden, w_out, w_dens, conv_w):
    block_count = lax.axis_size("blocks")
    segments = seg_feat.shape[2]
    color = render(
        block_count,
        seg_feat[0, 0],
        seg_block.reshape(1, segments),
        depth_rank[0, 0],
        w_in[0],
        w_hidden[0],
        w_out[0],
        w_dens,
    )
    tile_image = color.reshape(TH, TW, color.shape[1])
    rows_total = TH * lax.axis_size(("tiles", "sub"))
    cols_total = TW * block_count
    row_pos = (
        lax.axis_index(("tiles", "sub")) * TH
        - CONV_LAYERS
        + jnp.arange(TH + 2 * CONV_LAYERS, dtype=jnp.int32)
    )
    col_pos = (
        lax.axis_index("blocks") * TW
        - CONV_LAYERS
        + jnp.arange(TW + 2 * CONV_LAYERS, dtype=jnp.int32)
    )
    inside = ((row_pos >= 0) & (row_pos < rows_total))[:, None] & (
        (col_pos >= 0) & (col_pos < cols_total)
    )[None, :]
    current = with_halo(tile_image, (("blocks", 1), (("tiles", "sub"), 0)), CONV_LAYERS)
    for layer_index in range(CONV_LAYERS):
        margin = CONV_LAYERS - layer_index - 1
        size_h = TH + 2 * margin
        size_w = TW + 2 * margin
        current = conv_layer(current, conv_w[layer_index], size_h, size_w)
        keep_mask = inside[
            layer_index + 1 : layer_index + 1 + size_h, layer_index + 1 : layer_index + 1 + size_w
        ]
        current = jnp.where(keep_mask[:, :, None], current, jnp.zeros_like(current))
    tile_image = current
    return tile_image


def solution(mesh):
    in_specs = (
        P(("groups", "tiles", "sub"), "blocks", None, None),
        P(("groups", "tiles", "sub"), "blocks", None, None),
        P(("groups", "tiles", "sub"), "blocks", None, None),
        P("blocks", None, None),
        P("blocks", None, None, None),
        P("blocks", None, None),
        P("blocks", None),
        P(),
    )
    out_specs = P(("groups", "tiles", "sub"), "blocks", None)
    return jax.shard_map(shards, mesh=mesh, in_specs=in_specs, out_specs=out_specs, check_vma=False)
```

```python
import functools

import jax
import jax.numpy as jnp
from jax import lax
from jax.experimental import pallas as pl
from jax.experimental.pallas import tpu as pltpu
from jax.sharding import PartitionSpec as P

SEGS_RAY = 8
CONV_LAYERS = 3
TW = 16
TH = 16
RAYS_DEV = 256
MESH = pl.DeviceIdType.MESH
F32 = jnp.float32
BF16 = jnp.bfloat16


def silu(value):
    half = value * jnp.asarray(0.5, value.dtype)
    return half + half * jnp.tanh(half)


def softplus(value):
    return jnp.maximum(value, 0.0) + jnp.log1p(jnp.exp(-jnp.abs(value)))


def block_at(step, place, count):
    near = jnp.minimum(place, count - 1 - place)
    distance = (step + 1) // 2
    paired = jnp.where(step % 2 == 1, place + distance, place - distance)
    rest = jnp.where(2 * place <= count - 1, step, count - 1 - step)
    return jnp.where(step <= 2 * near, paired, rest)


AROUND = [(dy, dx) for dy in (-1, 0, 1) for dx in (-1, 0, 1) if (dy, dx) != (0, 0)]
Z, X, Y, D, SA, SX, SY, SD, ZD = range(9)


def render_kernel(
    count,
    tiles_count,
    capacity,
    row_tile,
    feat_ref,
    block_ref,
    rank_ref,
    w_in_ref,
    w_hid_ref,
    w_out_ref,
    w_dens_ref,
    color_ref,
    hid,
    ends,
    slot_row,
    wide,
    turns,
    rays,
    act,
    heads,
    dens_map,
    around,
    edge_send,
    edge_recv,
    send_sem,
    recv_sem,
    ends_send,
    ends_recv,
    own_sem,
):
    place = lax.axis_index("blocks")
    tile = lax.axis_index("tiles")
    group = lax.axis_index("groups")
    core = lax.axis_index("sub")
    tile_mate = tile + 1 - 2 * (tile % 2)
    group_mate = group + 1 - 2 * (group % 2)
    core_mate = 1 - core
    tx, gy = tile % 2, group % 2
    layers = w_hid_ref.shape[0]
    hidden = w_hid_ref.shape[2]
    part = hidden // 8
    end_rows = ends.shape[1]
    end_half = end_rows // 2
    feats = w_out_ref.shape[1]
    in_width = w_in_ref.shape[0]
    segments = feat_ref.shape[0]

    def eighth(a, b, c):
        return (a * 2 + b) * 2 + c

    to_x, to_y, to_c = {"tiles": tile_mate}, {"groups": group_mate}, {"sub": core_mate}

    line = tile * 2 + core
    lines = 2 * tiles_count

    def beside(dy, dx):
        row, column = line + dy, place + dx
        exists = 1
        if dy < 0:
            exists = exists * jnp.minimum(line, 1)
        if dy > 0:
            exists = exists * jnp.minimum(lines - 1 - line, 1)
        if dx < 0:
            exists = exists * jnp.minimum(place, 1)
        if dx > 0:
            exists = exists * jnp.minimum(count - 1 - place, 1)
        return {"tiles": (row + 2) // 2 - 1, "sub": (row + 2) % 2, "blocks": column}, exists

    barrier = pltpu.get_barrier_semaphore()
    pl.semaphore_signal(barrier, inc=1, device_id=to_x, device_id_type=MESH)
    pl.semaphore_signal(barrier, inc=1, device_id=to_y, device_id_type=MESH)
    pl.semaphore_signal(barrier, inc=1, device_id=to_c, device_id_type=MESH)

    @pl.when(place > 0)
    def _():
        pl.semaphore_signal(barrier, inc=1, device_id={"blocks": place - 1}, device_id_type=MESH)

    @pl.when(place < count - 1)
    def _():
        pl.semaphore_signal(barrier, inc=1, device_id={"blocks": place + 1}, device_id_type=MESH)

    around[...] = jnp.zeros_like(around)
    own = pltpu.make_async_copy(w_hid_ref, hid.at[place], own_sem)
    own.start()
    ends[place, 0:in_width] = w_in_ref[...]
    ends[place, in_width : in_width + feats] = w_out_ref[...].T
    ends[place, in_width + feats : end_rows] = jnp.broadcast_to(
        w_dens_ref[...], (end_rows - in_width - feats, hidden)
    )
    own.wait()

    peers = 3 + jnp.minimum(place, 1) + jnp.minimum(count - 1 - place, 1)
    for dy, dx in AROUND:
        there, exists = beside(dy, dx)

        @pl.when(exists == 1)
        def _():
            pl.semaphore_signal(barrier, inc=1, device_id=there, device_id_type=MESH)

        peers = peers + exists
    pl.semaphore_wait(barrier, peers)

    def piece(block, layer, which):
        return hid.at[block, layer, pl.ds(pl.multiple_of(which * part, part), part)]

    def move(block, layer, which, kind, target, send_kind=None):
        ref = piece(block, layer, which)
        return pltpu.make_async_remote_copy(
            src_ref=ref,
            dst_ref=ref,
            send_sem=send_sem.at[block, layer, kind if send_kind is None else send_kind],
            recv_sem=recv_sem.at[block, layer, kind],
            device_id=target,
            device_id_type=MESH,
        )

    def move_ends(block, half, kind, target, send_kind=None):
        ref = ends.at[block, pl.ds(pl.multiple_of(half * end_half, end_half), end_half)]
        return pltpu.make_async_remote_copy(
            src_ref=ref,
            dst_ref=ref,
            send_sem=ends_send.at[block, kind if send_kind is None else send_kind],
            recv_sem=ends_recv.at[block, kind],
            device_id=target,
            device_id_type=MESH,
        )

    e_own = eighth(tx, gy, core)
    e_x = eighth(1 - tx, gy, core)
    e_y = eighth(tx, 1 - gy, core)
    e_d = eighth(1 - tx, 1 - gy, core)
    m_own = eighth(tx, gy, core_mate)
    m_x = eighth(1 - tx, gy, core_mate)
    m_y = eighth(tx, 1 - gy, core_mate)
    m_d = eighth(1 - tx, 1 - gy, core_mate)
    up, down = {"blocks": place + 1}, {"blocks": place - 1}

    def own_up(action):
        @pl.when(place < count - 1)
        def _():
            action(move_ends(place, core, 0, up))
            for layer in range(layers):
                action(move(place, layer, e_own, Z, up))

    def own_down(action):
        @pl.when(place > 0)
        def _():
            action(move_ends(place, core, 0, down, 2))
            for layer in range(layers):
                action(move(place, layer, e_own, Z, down, ZD))

    own_up(lambda c: c.start())
    own_down(lambda c: c.start())

    def onward(block, action):
        @pl.when((block < place) & (place < count - 1))
        def _():
            action(up)

        @pl.when((block > place) & (place > 0))
        def _():
            action(down)

    def arrive(block, layer):
        move(block, layer, e_own, Z, up).wait_recv()
        onward(block, lambda to: move(block, layer, e_own, Z, to).start())
        move(block, layer, e_own, X, to_x).start()
        move(block, layer, e_own, Y, to_y).start()
        move(block, layer, e_own, SA, to_c).start()

    def arrive_ends(block):
        move_ends(block, core, 0, up).wait_recv()
        onward(block, lambda to: move_ends(block, core, 0, to).start())
        move_ends(block, core, 1, to_c).start()

    def cross(block, layer):
        move(block, layer, e_x, X, to_x).wait_recv()
        move(block, layer, e_y, Y, to_y).wait_recv()

        @pl.when(core == 0)
        def _():
            move(block, layer, e_x, D, to_y).start()

        @pl.when(core == 1)
        def _():
            move(block, layer, e_y, D, to_x).start()

        move(block, layer, e_x, SX, to_c).start()
        move(block, layer, e_y, SY, to_c).start()

    def corner(block, layer):
        move(block, layer, e_d, D, to_x).wait_recv()
        move(block, layer, e_d, SD, to_c).start()

    def ready(block, layer):
        move(block, layer, m_own, SA, to_c).wait_recv()
        move(block, layer, m_x, SX, to_c).wait_recv()
        move(block, layer, m_y, SY, to_c).wait_recv()
        move(block, layer, m_d, SD, to_c).wait_recv()

    def item(step, layer, ahead):
        return step + (layer + ahead) // layers, (layer + ahead) % layers

    def exchange(step, layer):
        for ahead, action in ((4, arrive), (3, cross), (2, corner)):
            later, its_layer = item(step, layer, ahead)

            @pl.when((later > 0) & (later < count))
            def _():
                block = block_at(later, place, count)
                if action is arrive and its_layer == 0:
                    arrive_ends(block)
                action(block, its_layer)

    rows16 = 16
    chunks = segments // 128
    lane = lax.broadcasted_iota(jnp.int32, (128, 128), 1)
    sub = lax.broadcasted_iota(jnp.int32, (128, 128), 0)
    earlier = (sub < lane).astype(F32).astype(BF16)
    names = lax.broadcasted_iota(jnp.int32, (rows16, 128), 0)
    base = names.astype(F32) * capacity
    named = [
        (jnp.broadcast_to(block_ref[:, c * 128 : (c + 1) * 128], (rows16, 128)) == names).astype(F32)
        for c in range(chunks)
    ]
    before = jnp.dot(
        jnp.concatenate(named, axis=0).astype(BF16), earlier, preferred_element_type=F32
    )
    carry = base
    for c in range(chunks):
        ahead_of = before[c * rows16 : (c + 1) * rows16] + carry
        carry = carry + jnp.sum(named[c], axis=1, keepdims=True)
        slot_row[:, c * 128 : (c + 1) * 128] = jnp.sum(named[c] * ahead_of, axis=0, keepdims=True)
    wide[:, 0:in_width] = feat_ref[...]
    ray_of = lax.broadcasted_iota(jnp.int32, (RAYS_DEV, 128), 0)
    lane_of = lax.broadcasted_iota(jnp.int32, (RAYS_DEV, 128), 1)
    ray_tag = jnp.where(lane_of == SEGS_RAY, ray_of, 0)
    for k in range(SEGS_RAY):
        tags = jnp.where(lane_of == k, 1, ray_tag)
        wide[k * RAYS_DEV : (k + 1) * RAYS_DEV, in_width : in_width + 128] = tags.astype(F32).astype(
            BF16
        )
    dens_map[...] = jnp.zeros_like(dens_map)

    pick_tile = min(256, capacity)

    def tile_loop(body, size):
        for index in range(capacity // size):
            body(slice(index * size, (index + 1) * size), index)

    rows_first = (((0,), (0,)), ((), ()))

    def gather_in(step, block):
        def body(rows, index):
            first = (block * capacity + index * pick_tile).astype(F32)
            held = jnp.clip(slot_row[...] - first, -1.0, float(pick_tile)).astype(BF16)
            wanted = lax.broadcasted_iota(jnp.int32, (pick_tile, segments), 0).astype(F32).astype(BF16)
            same = jnp.broadcast_to(held, (pick_tile, segments)) == wanted
            pick = jnp.where(same, jnp.ones((), BF16), jnp.zeros((), BF16))
            mine = jnp.dot(pick, wide[...], preferred_element_type=F32)
            tag = mine[:, in_width : in_width + 128]
            turns[step, rows] = jnp.where(lane_tile < SEGS_RAY, tag, 0.0).astype(BF16)
            on_ray = lax.broadcasted_iota(jnp.int32, (pick_tile, RAYS_DEV), 1).astype(F32)
            rays[step, rows] = (tag[:, SEGS_RAY : SEGS_RAY + 1] == on_ray).astype(F32).astype(BF16)
            act[rows] = silu(
                jnp.dot(
                    mine[:, 0:in_width].astype(BF16),
                    ends[block, 0:in_width],
                    preferred_element_type=F32,
                ).astype(BF16)
            )

        tile_loop(body, pick_tile)

    lane_tile = lax.broadcasted_iota(jnp.int32, (pick_tile, 128), 1)

    def layer_step(block, layer):
        def body(rows, index):
            value = act[rows]
            act[rows] = value + silu(
                jnp.dot(value, hid[block, layer], preferred_element_type=F32).astype(BF16)
            )

        tile_loop(body, row_tile)

    def head_step(step, block):
        w_den = jnp.broadcast_to(ends[block, in_width + feats : in_width + feats + 1], (128, hidden))
        w_head = jnp.concatenate([ends[block, in_width : in_width + feats], w_den], axis=0)
        contract = (((1,), (1,)), ((), ()))

        def body(rows, index):
            out = lax.dot_general(act[rows], w_head, contract, preferred_element_type=F32)
            heads[step, rows] = out[:, 0:feats].astype(BF16)
            density = (0.25 * softplus(out[:, feats : feats + 128])).astype(BF16)
            dens_map[...] += lax.dot_general(
                turns[step, rows] * density, rays[step, rows], rows_first, preferred_element_type=F32
            )

        tile_loop(body, row_tile)

    def step_body(step, carry_in):
        block = block_at(step, place, count)
        for layer in range(layers):
            exchange(step, layer)

            @pl.when(step > 0)
            def _():
                if layer == 0:
                    move_ends(block, core_mate, 1, to_c).wait_recv()
                ready(block, layer)

            if layer == 0:
                gather_in(step, block)
            layer_step(block, layer)
        head_step(step, block)
        return carry_in

    lax.fori_loop(0, count, step_body, 0)

    density = dens_map[0:SEGS_RAY]
    optical = jnp.zeros((SEGS_RAY, RAYS_DEV), F32)
    for k in range(SEGS_RAY):
        nearer = rank_ref[k : k + 1, :] < rank_ref[...]
        optical += jnp.where(nearer, density[k : k + 1], 0.0)
    weight = jnp.exp(-optical) * (1.0 - jnp.exp(-density))
    weight = jnp.concatenate([weight, jnp.zeros((128 - SEGS_RAY, RAYS_DEV), F32)], axis=0)
    weight = weight.astype(BF16)

    def blend(step, color):
        spread = jnp.dot(turns[step], weight, preferred_element_type=F32).astype(BF16) * rays[step]
        return color + lax.dot_general(heads[step], spread, rows_first, preferred_element_type=F32)

    color = lax.fori_loop(0, count, blend, jnp.zeros((feats, RAYS_DEV), F32))
    around[4] = color.T.astype(BF16)

    def strip(dy, dx):
        edge = CONV_LAYERS * TW
        rows = {0: (0, RAYS_DEV), -1: (0, edge), 1: (RAYS_DEV - edge, edge)}[dy]
        mine = around.at[4, pl.ds(*rows)]
        theirs = around.at[(1 - dy) * 3 + 1 - dx, pl.ds(*rows)]
        return mine, theirs

    def edge_copy(index, dy, dx):
        mine, theirs = strip(dy, dx)
        there, exists = beside(dy, dx)
        return exists, pltpu.make_async_remote_copy(
            src_ref=mine,
            dst_ref=theirs,
            send_sem=edge_send.at[index],
            recv_sem=edge_recv.at[index],
            device_id=there,
            device_id_type=MESH,
        )

    for index, (dy, dx) in enumerate(AROUND):
        exists, copy = edge_copy(index, dy, dx)

        @pl.when(exists == 1)
        def _():
            copy.start()

    for index, (dy, dx) in enumerate(AROUND):
        _, arriving = edge_copy(index, dy, dx)
        _, from_there = beside(-dy, -dx)

        @pl.when(from_there == 1)
        def _():
            arriving.wait_recv()

        exists, copy = edge_copy(index, dy, dx)

        @pl.when(exists == 1)
        def _():
            copy.wait_send()

    color_ref[...] = around[...]

    own_up(lambda c: c.wait_send())
    own_down(lambda c: c.wait_send())

    def drain(step, carry_in):
        block = block_at(step, place, count)
        onward(block, lambda to: move_ends(block, core, 0, to).wait_send())
        move_ends(block, core, 1, to_c).wait_send()
        for layer in range(layers):
            onward(block, lambda to, layer=layer: move(block, layer, e_own, Z, to).wait_send())
            for kind in (X, Y, D, SA, SX, SY, SD):
                move(block, layer, e_own, kind, to_c).wait_send()
        return carry_in

    lax.fori_loop(1, count, drain, 0)


def render(count, tiles_count, rows, block_ids, ranks, w_in, w_hid, w_out, w_dens):
    segments, in_width = rows.shape
    capacity = 2 * segments // count
    layers, hidden, _ = w_hid.shape
    feats = w_out.shape[1]
    row_tile = min(512, capacity)
    end_rows = in_width + feats + 32
    vmem = pl.BlockSpec(memory_space=pltpu.VMEM)
    macs = count * capacity * hidden * (in_width + layers * hidden + feats)
    return pl.pallas_call(
        functools.partial(render_kernel, count, tiles_count, capacity, row_tile),
        out_shape=jax.ShapeDtypeStruct((9, RAYS_DEV, feats), BF16),
        in_specs=[vmem, vmem, vmem, vmem, pl.BlockSpec(memory_space=pl.ANY), vmem, vmem],
        out_specs=vmem,
        scratch_shapes=[
            pltpu.VMEM((count, layers, hidden, hidden), BF16),
            pltpu.VMEM((count, end_rows, hidden), BF16),
            pltpu.VMEM((1, segments), F32),
            pltpu.VMEM((segments, in_width + 128), BF16),
            pltpu.VMEM((count, capacity, 128), BF16),
            pltpu.VMEM((count, capacity, RAYS_DEV), BF16),
            pltpu.VMEM((capacity, hidden), BF16),
            pltpu.VMEM((count, capacity, feats), BF16),
            pltpu.VMEM((128, RAYS_DEV), F32),
            pltpu.VMEM((9, RAYS_DEV, feats), BF16),
            pltpu.SemaphoreType.DMA((8,)),
            pltpu.SemaphoreType.DMA((8,)),
            pltpu.SemaphoreType.DMA((count, layers, 9)),
            pltpu.SemaphoreType.DMA((count, layers, 8)),
            pltpu.SemaphoreType.DMA((count, 3)),
            pltpu.SemaphoreType.DMA((count, 2)),
            pltpu.SemaphoreType.DMA,
        ],
        compiler_params=pltpu.CompilerParams(
            collective_id=0, has_side_effects=True, vmem_limit_bytes=56 * 1024 * 1024
        ),
        cost_estimate=pl.CostEstimate(flops=2 * macs, bytes_accessed=4 << 20, transcendentals=0),
        name="render",
    )(rows, block_ids, ranks, w_in, w_hid, w_out, w_dens)


def conv_layer(padded, kernel, out_rows, out_cols):
    pieces = []
    for offset_y in range(3):
        for offset_x in range(3):
            pieces.append(padded[offset_y : offset_y + out_rows, offset_x : offset_x + out_cols])
    patches = jnp.concatenate(pieces, axis=-1)
    channels = kernel.shape[-1]
    result = jnp.dot(
        patches, kernel.reshape(9 * kernel.shape[2], channels), preferred_element_type=jnp.float32
    )
    center = padded[1 : 1 + out_rows, 1 : 1 + out_cols].astype(jnp.float32)
    return (center + jax.nn.silu(result)).astype(jnp.bfloat16)


def shards(seg_feat, seg_block, depth_rank, w_in, w_hidden, w_out, w_dens, conv_w):
    block_count = lax.axis_size("blocks")
    segments = seg_feat.shape[2]
    color = render(
        block_count,
        lax.axis_size("tiles"),
        seg_feat[0, 0],
        seg_block.reshape(1, segments),
        depth_rank[0, 0],
        w_in[0],
        w_hidden[0],
        w_out[0],
        w_dens,
    )
    feats = color.shape[2]
    grid = color.reshape(3, 3, TH, TW, feats)
    last = {0: slice(TH - CONV_LAYERS, TH), 1: slice(0, TH), 2: slice(0, CONV_LAYERS)}
    tile_image = jnp.concatenate(
        [
            jnp.concatenate([grid[a, b, last[a], last[b]] for b in range(3)], axis=1)
            for a in range(3)
        ],
        axis=0,
    )
    rows_total = TH * lax.axis_size(("tiles", "sub"))
    cols_total = TW * block_count
    row_pos = (
        lax.axis_index(("tiles", "sub")) * TH
        - CONV_LAYERS
        + jnp.arange(TH + 2 * CONV_LAYERS, dtype=jnp.int32)
    )
    col_pos = (
        lax.axis_index("blocks") * TW
        - CONV_LAYERS
        + jnp.arange(TW + 2 * CONV_LAYERS, dtype=jnp.int32)
    )
    inside = ((row_pos >= 0) & (row_pos < rows_total))[:, None] & (
        (col_pos >= 0) & (col_pos < cols_total)
    )[None, :]
    current = tile_image
    for layer_index in range(CONV_LAYERS):
        margin = CONV_LAYERS - layer_index - 1
        size_h = TH + 2 * margin
        size_w = TW + 2 * margin
        current = conv_layer(current, conv_w[layer_index], size_h, size_w)
        keep_mask = inside[
            layer_index + 1 : layer_index + 1 + size_h, layer_index + 1 : layer_index + 1 + size_w
        ]
        current = jnp.where(keep_mask[:, :, None], current, jnp.zeros_like(current))
    tile_image = current
    return tile_image


def solution(mesh):
    in_specs = (
        P(("groups", "tiles", "sub"), "blocks", None, None),
        P(("groups", "tiles", "sub"), "blocks", None, None),
        P(("groups", "tiles", "sub"), "blocks", None, None),
        P("blocks", None, None),
        P("blocks", None, None, None),
        P("blocks", None, None),
        P("blocks", None),
        P(),
    )
    out_specs = P(("groups", "tiles", "sub"), "blocks", None)
    return jax.shard_map(shards, mesh=mesh, in_specs=in_specs, out_specs=out_specs, check_vma=False)
```

```python
import functools

import jax
import jax.numpy as jnp
from jax import lax
from jax.experimental import pallas as pl
from jax.experimental.pallas import tpu as pltpu
from jax.sharding import PartitionSpec as P

SEGS_RAY = 8
CONV_LAYERS = 3
TW = 16
TH = 16
RAYS_DEV = 256
MESH = pl.DeviceIdType.MESH
F32 = jnp.float32
BF16 = jnp.bfloat16


def silu(value):
    half = value * jnp.asarray(0.5, value.dtype)
    return half + half * jnp.tanh(half)


def softplus(value):
    return jnp.maximum(value, 0.0) + jnp.log1p(jnp.exp(-jnp.abs(value)))


def block_at(step, place, count):
    near = jnp.minimum(place, count - 1 - place)
    distance = (step + 1) // 2
    paired = jnp.where(step % 2 == 1, place + distance, place - distance)
    rest = jnp.where(2 * place <= count - 1, step, count - 1 - step)
    return jnp.where(step <= 2 * near, paired, rest)


BUNDLE = 2
AROUND = [(dy, dx) for dy in (-1, 0, 1) for dx in (-1, 0, 1) if (dy, dx) != (0, 0)]
Z, X, Y, D, SA, SX, SY, SD, ZD = range(9)


def render_kernel(
    count,
    tiles_count,
    capacity,
    row_tile,
    feat_ref,
    block_ref,
    rank_ref,
    w_in_ref,
    w_hid_ref,
    w_out_ref,
    w_dens_ref,
    color_ref,
    hid,
    ends,
    slot_row,
    wide,
    turns,
    rays,
    act,
    heads,
    dens_map,
    around,
    edge_send,
    edge_recv,
    send_sem,
    recv_sem,
    ends_send,
    ends_recv,
    own_sem,
):
    place = lax.axis_index("blocks")
    tile = lax.axis_index("tiles")
    group = lax.axis_index("groups")
    core = lax.axis_index("sub")
    tile_mate = tile + 1 - 2 * (tile % 2)
    group_mate = group + 1 - 2 * (group % 2)
    core_mate = 1 - core
    tx, gy = tile % 2, group % 2
    layers = w_hid_ref.shape[0]
    hidden = w_hid_ref.shape[2]
    bundles = layers // BUNDLE
    part = hidden // 8
    end_rows = ends.shape[1]
    end_half = end_rows // 2
    feats = w_out_ref.shape[1]
    in_width = w_in_ref.shape[0]
    segments = feat_ref.shape[0]

    def eighth(a, b, c):
        return (a * 2 + b) * 2 + c

    to_x, to_y, to_c = {"tiles": tile_mate}, {"groups": group_mate}, {"sub": core_mate}

    line = tile * 2 + core
    lines = 2 * tiles_count

    def beside(dy, dx):
        row, column = line + dy, place + dx
        exists = 1
        if dy < 0:
            exists = exists * jnp.minimum(line, 1)
        if dy > 0:
            exists = exists * jnp.minimum(lines - 1 - line, 1)
        if dx < 0:
            exists = exists * jnp.minimum(place, 1)
        if dx > 0:
            exists = exists * jnp.minimum(count - 1 - place, 1)
        return {"tiles": (row + 2) // 2 - 1, "sub": (row + 2) % 2, "blocks": column}, exists

    barrier = pltpu.get_barrier_semaphore()
    pl.semaphore_signal(barrier, inc=1, device_id=to_x, device_id_type=MESH)
    pl.semaphore_signal(barrier, inc=1, device_id=to_y, device_id_type=MESH)
    pl.semaphore_signal(barrier, inc=1, device_id=to_c, device_id_type=MESH)

    @pl.when(place > 0)
    def _():
        pl.semaphore_signal(barrier, inc=1, device_id={"blocks": place - 1}, device_id_type=MESH)

    @pl.when(place < count - 1)
    def _():
        pl.semaphore_signal(barrier, inc=1, device_id={"blocks": place + 1}, device_id_type=MESH)

    around[...] = jnp.zeros_like(around)
    own = pltpu.make_async_copy(w_hid_ref, hid.at[place], own_sem)
    own.start()
    ends[place, 0:in_width] = w_in_ref[...]
    ends[place, in_width : in_width + feats] = w_out_ref[...].T
    ends[place, in_width + feats : end_rows] = jnp.broadcast_to(
        w_dens_ref[...], (end_rows - in_width - feats, hidden)
    )
    own.wait()

    peers = 3 + jnp.minimum(place, 1) + jnp.minimum(count - 1 - place, 1)
    for dy, dx in AROUND:
        there, exists = beside(dy, dx)

        @pl.when(exists == 1)
        def _():
            pl.semaphore_signal(barrier, inc=1, device_id=there, device_id_type=MESH)

        peers = peers + exists
    pl.semaphore_wait(barrier, peers)

    def piece(block, layer, which):
        return hid.at[
            block, pl.ds(layer * BUNDLE, BUNDLE), pl.ds(pl.multiple_of(which * part, part), part)
        ]

    def move(block, layer, which, kind, target, send_kind=None):
        ref = piece(block, layer, which)
        return pltpu.make_async_remote_copy(
            src_ref=ref,
            dst_ref=ref,
            send_sem=send_sem.at[block, layer, kind if send_kind is None else send_kind],
            recv_sem=recv_sem.at[block, layer, kind],
            device_id=target,
            device_id_type=MESH,
        )

    def move_ends(block, half, kind, target, send_kind=None):
        ref = ends.at[block, pl.ds(pl.multiple_of(half * end_half, end_half), end_half)]
        return pltpu.make_async_remote_copy(
            src_ref=ref,
            dst_ref=ref,
            send_sem=ends_send.at[block, kind if send_kind is None else send_kind],
            recv_sem=ends_recv.at[block, kind],
            device_id=target,
            device_id_type=MESH,
        )

    e_own = eighth(tx, gy, core)
    e_x = eighth(1 - tx, gy, core)
    e_y = eighth(tx, 1 - gy, core)
    e_d = eighth(1 - tx, 1 - gy, core)
    m_own = eighth(tx, gy, core_mate)
    m_x = eighth(1 - tx, gy, core_mate)
    m_y = eighth(tx, 1 - gy, core_mate)
    m_d = eighth(1 - tx, 1 - gy, core_mate)
    up, down = {"blocks": place + 1}, {"blocks": place - 1}

    def own_up(action):
        @pl.when(place < count - 1)
        def _():
            action(move_ends(place, core, 0, up))
            for layer in range(bundles):
                action(move(place, layer, e_own, Z, up))

    def own_down(action):
        @pl.when(place > 0)
        def _():
            action(move_ends(place, core, 0, down, 2))
            for layer in range(bundles):
                action(move(place, layer, e_own, Z, down, ZD))

    own_up(lambda c: c.start())
    own_down(lambda c: c.start())

    def onward(block, action):
        @pl.when((block < place) & (place < count - 1))
        def _():
            action(up)

        @pl.when((block > place) & (place > 0))
        def _():
            action(down)

    def arrive(block, layer):
        move(block, layer, e_own, Z, up).wait_recv()
        onward(block, lambda to: move(block, layer, e_own, Z, to).start())
        move(block, layer, e_own, X, to_x).start()
        move(block, layer, e_own, Y, to_y).start()
        move(block, layer, e_own, SA, to_c).start()

    def arrive_ends(block):
        move_ends(block, core, 0, up).wait_recv()
        onward(block, lambda to: move_ends(block, core, 0, to).start())
        move_ends(block, core, 1, to_c).start()

    def cross(block, layer):
        move(block, layer, e_x, X, to_x).wait_recv()
        move(block, layer, e_y, Y, to_y).wait_recv()

        @pl.when(core == 0)
        def _():
            move(block, layer, e_x, D, to_y).start()

        @pl.when(core == 1)
        def _():
            move(block, layer, e_y, D, to_x).start()

        move(block, layer, e_x, SX, to_c).start()
        move(block, layer, e_y, SY, to_c).start()

    def corner(block, layer):
        move(block, layer, e_d, D, to_x).wait_recv()
        move(block, layer, e_d, SD, to_c).start()

    def ready(block, layer):
        move(block, layer, m_own, SA, to_c).wait_recv()
        move(block, layer, m_x, SX, to_c).wait_recv()
        move(block, layer, m_y, SY, to_c).wait_recv()
        move(block, layer, m_d, SD, to_c).wait_recv()

    def item(step, layer, ahead):
        return step + (layer + ahead) // layers, (layer + ahead) % layers

    def exchange(step, layer):
        for ahead, action in ((1, corner), (2, cross), (4, arrive)):
            later, its_layer = item(step, layer, ahead)
            if its_layer % BUNDLE:
                continue

            @pl.when((later > 0) & (later < count))
            def _():
                block = block_at(later, place, count)
                if action is arrive and its_layer == 0:
                    arrive_ends(block)
                action(block, its_layer // BUNDLE)

    rows16 = 16
    chunks = segments // 128
    lane = lax.broadcasted_iota(jnp.int32, (128, 128), 1)
    sub = lax.broadcasted_iota(jnp.int32, (128, 128), 0)
    earlier = (sub < lane).astype(F32).astype(BF16)
    names = lax.broadcasted_iota(jnp.int32, (rows16, 128), 0)
    base = names.astype(F32) * capacity
    named = [
        (jnp.broadcast_to(block_ref[:, c * 128 : (c + 1) * 128], (rows16, 128)) == names).astype(F32)
        for c in range(chunks)
    ]
    before = jnp.dot(
        jnp.concatenate(named, axis=0).astype(BF16), earlier, preferred_element_type=F32
    )
    carry = base
    for c in range(chunks):
        ahead_of = before[c * rows16 : (c + 1) * rows16] + carry
        carry = carry + jnp.sum(named[c], axis=1, keepdims=True)
        slot_row[:, c * 128 : (c + 1) * 128] = jnp.sum(named[c] * ahead_of, axis=0, keepdims=True)
    wide[:, 0:in_width] = feat_ref[...]
    ray_of = lax.broadcasted_iota(jnp.int32, (RAYS_DEV, 128), 0)
    lane_of = lax.broadcasted_iota(jnp.int32, (RAYS_DEV, 128), 1)
    ray_tag = jnp.where(lane_of == SEGS_RAY, ray_of, 0)
    for k in range(SEGS_RAY):
        tags = jnp.where(lane_of == k, 1, ray_tag)
        wide[k * RAYS_DEV : (k + 1) * RAYS_DEV, in_width : in_width + 128] = tags.astype(F32).astype(
            BF16
        )
    dens_map[...] = jnp.zeros_like(dens_map)

    pick_tile = min(256, capacity)

    def tile_loop(body, size):
        for index in range(capacity // size):
            body(slice(index * size, (index + 1) * size), index)

    rows_first = (((0,), (0,)), ((), ()))

    def gather_in(step, block):
        def body(rows, index):
            first = (block * capacity + index * pick_tile).astype(F32)
            held = jnp.clip(slot_row[...] - first, -1.0, float(pick_tile)).astype(BF16)
            wanted = lax.broadcasted_iota(jnp.int32, (pick_tile, segments), 0).astype(F32).astype(BF16)
            same = jnp.broadcast_to(held, (pick_tile, segments)) == wanted
            pick = jnp.where(same, jnp.ones((), BF16), jnp.zeros((), BF16))
            mine = jnp.dot(pick, wide[...], preferred_element_type=F32)
            tag = mine[:, in_width : in_width + 128]
            turns[step, rows] = jnp.where(lane_tile < SEGS_RAY, tag, 0.0).astype(BF16)
            on_ray = lax.broadcasted_iota(jnp.int32, (pick_tile, RAYS_DEV), 1).astype(F32)
            rays[step, rows] = (tag[:, SEGS_RAY : SEGS_RAY + 1] == on_ray).astype(F32).astype(BF16)
            act[rows] = silu(
                jnp.dot(
                    mine[:, 0:in_width].astype(BF16),
                    ends[block, 0:in_width],
                    preferred_element_type=F32,
                ).astype(BF16)
            )

        tile_loop(body, pick_tile)

    lane_tile = lax.broadcasted_iota(jnp.int32, (pick_tile, 128), 1)

    def layer_step(block, layer):
        def body(rows, index):
            value = act[rows]
            act[rows] = value + silu(
                jnp.dot(value, hid[block, layer], preferred_element_type=F32).astype(BF16)
            )

        tile_loop(body, row_tile)

    def head_step(step, block):
        w_den = jnp.broadcast_to(ends[block, in_width + feats : in_width + feats + 1], (128, hidden))
        w_head = jnp.concatenate([ends[block, in_width : in_width + feats], w_den], axis=0)
        contract = (((1,), (1,)), ((), ()))

        def body(rows, index):
            out = lax.dot_general(act[rows], w_head, contract, preferred_element_type=F32)
            heads[step, rows] = out[:, 0:feats].astype(BF16)
            density = (0.25 * softplus(out[:, feats : feats + 128])).astype(BF16)
            dens_map[...] += lax.dot_general(
                turns[step, rows] * density, rays[step, rows], rows_first, preferred_element_type=F32
            )

        tile_loop(body, row_tile)

    def step_body(step, carry_in):
        block = block_at(step, place, count)
        for layer in range(layers):
            exchange(step, layer)

            @pl.when(step > 0)
            def _():
                if layer == 0:
                    move_ends(block, core_mate, 1, to_c).wait_recv()
                if layer % BUNDLE == 0:
                    ready(block, layer // BUNDLE)

            if layer == 0:
                gather_in(step, block)
            layer_step(block, layer)
        head_step(step, block)
        return carry_in

    lax.fori_loop(0, count, step_body, 0)

    density = dens_map[0:SEGS_RAY]
    optical = jnp.zeros((SEGS_RAY, RAYS_DEV), F32)
    for k in range(SEGS_RAY):
        nearer = rank_ref[k : k + 1, :] < rank_ref[...]
        optical += jnp.where(nearer, density[k : k + 1], 0.0)
    weight = jnp.exp(-optical) * (1.0 - jnp.exp(-density))
    weight = jnp.concatenate([weight, jnp.zeros((128 - SEGS_RAY, RAYS_DEV), F32)], axis=0)
    weight = weight.astype(BF16)

    def blend(step, color):
        spread = jnp.dot(turns[step], weight, preferred_element_type=F32).astype(BF16) * rays[step]
        return color + lax.dot_general(heads[step], spread, rows_first, preferred_element_type=F32)

    color = lax.fori_loop(0, count, blend, jnp.zeros((feats, RAYS_DEV), F32))
    around[4] = color.T.astype(BF16)

    def strip(dy, dx):
        edge = CONV_LAYERS * TW
        rows = {0: (0, RAYS_DEV), -1: (0, edge), 1: (RAYS_DEV - edge, edge)}[dy]
        mine = around.at[4, pl.ds(*rows)]
        theirs = around.at[(1 - dy) * 3 + 1 - dx, pl.ds(*rows)]
        return mine, theirs

    def edge_copy(index, dy, dx):
        mine, theirs = strip(dy, dx)
        there, exists = beside(dy, dx)
        return exists, pltpu.make_async_remote_copy(
            src_ref=mine,
            dst_ref=theirs,
            send_sem=edge_send.at[index],
            recv_sem=edge_recv.at[index],
            device_id=there,
            device_id_type=MESH,
        )

    for index, (dy, dx) in enumerate(AROUND):
        exists, copy = edge_copy(index, dy, dx)

        @pl.when(exists == 1)
        def _():
            copy.start()

    for index, (dy, dx) in enumerate(AROUND):
        _, arriving = edge_copy(index, dy, dx)
        _, from_there = beside(-dy, -dx)

        @pl.when(from_there == 1)
        def _():
            arriving.wait_recv()

        exists, copy = edge_copy(index, dy, dx)

        @pl.when(exists == 1)
        def _():
            copy.wait_send()

    color_ref[...] = around[...]

    own_up(lambda c: c.wait_send())
    own_down(lambda c: c.wait_send())

    def drain(step, carry_in):
        block = block_at(step, place, count)
        onward(block, lambda to: move_ends(block, core, 0, to).wait_send())
        move_ends(block, core, 1, to_c).wait_send()
        for layer in range(bundles):
            onward(block, lambda to, layer=layer: move(block, layer, e_own, Z, to).wait_send())
            for kind in (X, Y, D, SA, SX, SY, SD):
                move(block, layer, e_own, kind, to_c).wait_send()
        return carry_in

    lax.fori_loop(1, count, drain, 0)


def render(count, tiles_count, rows, block_ids, ranks, w_in, w_hid, w_out, w_dens):
    segments, in_width = rows.shape
    capacity = 2 * segments // count
    layers, hidden, _ = w_hid.shape
    feats = w_out.shape[1]
    row_tile = min(512, capacity)
    end_rows = in_width + feats + 32
    vmem = pl.BlockSpec(memory_space=pltpu.VMEM)
    macs = count * capacity * hidden * (in_width + layers * hidden + feats)
    return pl.pallas_call(
        functools.partial(render_kernel, count, tiles_count, capacity, row_tile),
        out_shape=jax.ShapeDtypeStruct((9, RAYS_DEV, feats), BF16),
        in_specs=[vmem, vmem, vmem, vmem, pl.BlockSpec(memory_space=pl.ANY), vmem, vmem],
        out_specs=vmem,
        scratch_shapes=[
            pltpu.VMEM((count, layers, hidden, hidden), BF16),
            pltpu.VMEM((count, end_rows, hidden), BF16),
            pltpu.VMEM((1, segments), F32),
            pltpu.VMEM((segments, in_width + 128), BF16),
            pltpu.VMEM((count, capacity, 128), BF16),
            pltpu.VMEM((count, capacity, RAYS_DEV), BF16),
            pltpu.VMEM((capacity, hidden), BF16),
            pltpu.VMEM((count, capacity, feats), BF16),
            pltpu.VMEM((128, RAYS_DEV), F32),
            pltpu.VMEM((9, RAYS_DEV, feats), BF16),
            pltpu.SemaphoreType.DMA((8,)),
            pltpu.SemaphoreType.DMA((8,)),
            pltpu.SemaphoreType.DMA((count, layers // BUNDLE, 9)),
            pltpu.SemaphoreType.DMA((count, layers // BUNDLE, 8)),
            pltpu.SemaphoreType.DMA((count, 3)),
            pltpu.SemaphoreType.DMA((count, 2)),
            pltpu.SemaphoreType.DMA,
        ],
        compiler_params=pltpu.CompilerParams(
            collective_id=0, has_side_effects=True, vmem_limit_bytes=56 * 1024 * 1024
        ),
        cost_estimate=pl.CostEstimate(flops=2 * macs, bytes_accessed=4 << 20, transcendentals=0),
        name="render",
    )(rows, block_ids, ranks, w_in, w_hid, w_out, w_dens)


def conv_layer(padded, kernel, out_rows, out_cols):
    pieces = []
    for offset_y in range(3):
        for offset_x in range(3):
            pieces.append(padded[offset_y : offset_y + out_rows, offset_x : offset_x + out_cols])
    patches = jnp.concatenate(pieces, axis=-1)
    channels = kernel.shape[-1]
    result = jnp.dot(
        patches, kernel.reshape(9 * kernel.shape[2], channels), preferred_element_type=jnp.float32
    )
    center = padded[1 : 1 + out_rows, 1 : 1 + out_cols].astype(jnp.float32)
    return (center + jax.nn.silu(result)).astype(jnp.bfloat16)


def shards(seg_feat, seg_block, depth_rank, w_in, w_hidden, w_out, w_dens, conv_w):
    block_count = lax.axis_size("blocks")
    segments = seg_feat.shape[2]
    color = render(
        block_count,
        lax.axis_size("tiles"),
        seg_feat[0, 0],
        seg_block.reshape(1, segments),
        depth_rank[0, 0],
        w_in[0],
        w_hidden[0],
        w_out[0],
        w_dens,
    )
    feats = color.shape[2]
    grid = color.reshape(3, 3, TH, TW, feats)
    last = {0: slice(TH - CONV_LAYERS, TH), 1: slice(0, TH), 2: slice(0, CONV_LAYERS)}
    tile_image = jnp.concatenate(
        [
            jnp.concatenate([grid[a, b, last[a], last[b]] for b in range(3)], axis=1)
            for a in range(3)
        ],
        axis=0,
    )
    rows_total = TH * lax.axis_size(("tiles", "sub"))
    cols_total = TW * block_count
    row_pos = (
        lax.axis_index(("tiles", "sub")) * TH
        - CONV_LAYERS
        + jnp.arange(TH + 2 * CONV_LAYERS, dtype=jnp.int32)
    )
    col_pos = (
        lax.axis_index("blocks") * TW
        - CONV_LAYERS
        + jnp.arange(TW + 2 * CONV_LAYERS, dtype=jnp.int32)
    )
    inside = ((row_pos >= 0) & (row_pos < rows_total))[:, None] & (
        (col_pos >= 0) & (col_pos < cols_total)
    )[None, :]
    current = tile_image
    for layer_index in range(CONV_LAYERS):
        margin = CONV_LAYERS - layer_index - 1
        size_h = TH + 2 * margin
        size_w = TW + 2 * margin
        current = conv_layer(current, conv_w[layer_index], size_h, size_w)
        keep_mask = inside[
            layer_index + 1 : layer_index + 1 + size_h, layer_index + 1 : layer_index + 1 + size_w
        ]
        current = jnp.where(keep_mask[:, :, None], current, jnp.zeros_like(current))
    tile_image = current
    return tile_image


def solution(mesh):
    in_specs = (
        P(("groups", "tiles", "sub"), "blocks", None, None),
        P(("groups", "tiles", "sub"), "blocks", None, None),
        P(("groups", "tiles", "sub"), "blocks", None, None),
        P("blocks", None, None),
        P("blocks", None, None, None),
        P("blocks", None, None),
        P("blocks", None),
        P(),
    )
    out_specs = P(("groups", "tiles", "sub"), "blocks", None)
    return jax.shard_map(shards, mesh=mesh, in_specs=in_specs, out_specs=out_specs, check_vma=False)
```

```python
import functools

import jax
import jax.numpy as jnp
from jax import lax
from jax.experimental import pallas as pl
from jax.experimental.pallas import tpu as pltpu
from jax.sharding import PartitionSpec as P

SEGS_RAY = 8
CONV_LAYERS = 3
TW = 16
TH = 16
RAYS_DEV = 256
MESH = pl.DeviceIdType.MESH
F32 = jnp.float32
BF16 = jnp.bfloat16


def silu(value):
    half = value * jnp.asarray(0.5, value.dtype)
    return half + half * jnp.tanh(half)


def softplus(value):
    return jnp.maximum(value, 0.0) + jnp.log1p(jnp.exp(-jnp.abs(value)))


def block_at(step, place, count):
    near = jnp.minimum(place, count - 1 - place)
    distance = (step + 1) // 2
    paired = jnp.where(step % 2 == 1, place + distance, place - distance)
    rest = jnp.where(2 * place <= count - 1, step, count - 1 - step)
    return jnp.where(step <= 2 * near, paired, rest)


BUNDLE = 2
AROUND = [(dy, dx) for dy in (-1, 0, 1) for dx in (-1, 0, 1) if (dy, dx) != (0, 0)]
Z, X, Y, D, SA, SX, SY, SD, ZD = range(9)


def render_kernel(
    count,
    tiles_count,
    capacity,
    row_tile,
    feat_ref,
    block_ref,
    rank_ref,
    w_in_ref,
    w_hid_ref,
    w_out_ref,
    w_dens_ref,
    color_ref,
    hid,
    ends,
    slot_row,
    wide,
    turns,
    rays,
    act,
    heads,
    dens_map,
    around,
    edge_send,
    edge_recv,
    send_sem,
    recv_sem,
    ends_send,
    ends_recv,
    own_sem,
):
    place = lax.axis_index("blocks")
    tile = lax.axis_index("tiles")
    group = lax.axis_index("groups")
    core = lax.axis_index("sub")
    tile_mate = tile + 1 - 2 * (tile % 2)
    group_mate = group + 1 - 2 * (group % 2)
    core_mate = 1 - core
    tx, gy = tile % 2, group % 2
    layers = w_hid_ref.shape[0]
    hidden = w_hid_ref.shape[2]
    bundles = layers // BUNDLE
    part = hidden // 8
    end_rows = ends.shape[1]
    end_half = end_rows // 2
    feats = w_out_ref.shape[1]
    in_width = w_in_ref.shape[0]
    segments = feat_ref.shape[0]

    def eighth(a, b, c):
        return (a * 2 + b) * 2 + c

    to_x, to_y, to_c = {"tiles": tile_mate}, {"groups": group_mate}, {"sub": core_mate}

    line = tile * 2 + core
    lines = 2 * tiles_count

    def beside(dy, dx):
        row, column = line + dy, place + dx
        exists = 1
        if dy < 0:
            exists = exists * jnp.minimum(line, 1)
        if dy > 0:
            exists = exists * jnp.minimum(lines - 1 - line, 1)
        if dx < 0:
            exists = exists * jnp.minimum(place, 1)
        if dx > 0:
            exists = exists * jnp.minimum(count - 1 - place, 1)
        return {"tiles": (row + 2) // 2 - 1, "sub": (row + 2) % 2, "blocks": column}, exists

    barrier = pltpu.get_barrier_semaphore()
    pl.semaphore_signal(barrier, inc=1, device_id=to_x, device_id_type=MESH)
    pl.semaphore_signal(barrier, inc=1, device_id=to_y, device_id_type=MESH)
    pl.semaphore_signal(barrier, inc=1, device_id=to_c, device_id_type=MESH)

    @pl.when(place > 0)
    def _():
        pl.semaphore_signal(barrier, inc=1, device_id={"blocks": place - 1}, device_id_type=MESH)

    @pl.when(place < count - 1)
    def _():
        pl.semaphore_signal(barrier, inc=1, device_id={"blocks": place + 1}, device_id_type=MESH)

    around[...] = jnp.zeros_like(around)
    own = pltpu.make_async_copy(w_hid_ref, hid.at[place], own_sem)
    own.start()
    ends[place, 0:in_width] = w_in_ref[...]
    ends[place, in_width : in_width + feats] = w_out_ref[...].T
    ends[place, in_width + feats : end_rows] = jnp.broadcast_to(
        w_dens_ref[...], (end_rows - in_width - feats, hidden)
    )
    own.wait()

    peers = 3 + jnp.minimum(place, 1) + jnp.minimum(count - 1 - place, 1)
    for dy, dx in AROUND:
        there, exists = beside(dy, dx)

        @pl.when(exists == 1)
        def _():
            pl.semaphore_signal(barrier, inc=1, device_id=there, device_id_type=MESH)

        peers = peers + exists
    pl.semaphore_wait(barrier, peers)

    def piece(block, layer, which):
        return hid.at[
            block, pl.ds(layer * BUNDLE, BUNDLE), pl.ds(pl.multiple_of(which * part, part), part)
        ]

    def move(block, layer, which, kind, target, send_kind=None):
        ref = piece(block, layer, which)
        return pltpu.make_async_remote_copy(
            src_ref=ref,
            dst_ref=ref,
            send_sem=send_sem.at[block, layer, kind if send_kind is None else send_kind],
            recv_sem=recv_sem.at[block, layer, kind],
            device_id=target,
            device_id_type=MESH,
        )

    def move_ends(block, half, kind, target, send_kind=None):
        ref = ends.at[block, pl.ds(pl.multiple_of(half * end_half, end_half), end_half)]
        return pltpu.make_async_remote_copy(
            src_ref=ref,
            dst_ref=ref,
            send_sem=ends_send.at[block, kind if send_kind is None else send_kind],
            recv_sem=ends_recv.at[block, kind],
            device_id=target,
            device_id_type=MESH,
        )

    e_own = eighth(tx, gy, core)
    e_x = eighth(1 - tx, gy, core)
    e_y = eighth(tx, 1 - gy, core)
    e_d = eighth(1 - tx, 1 - gy, core)
    m_own = eighth(tx, gy, core_mate)
    m_x = eighth(1 - tx, gy, core_mate)
    m_y = eighth(tx, 1 - gy, core_mate)
    m_d = eighth(1 - tx, 1 - gy, core_mate)
    up, down = {"blocks": place + 1}, {"blocks": place - 1}

    def own_moves(action):
        def both(make):
            @pl.when(place < count - 1)
            def _():
                action(make(up, None))

            @pl.when(place > 0)
            def _():
                action(make(down, True))

        def bundle_move(bundle):
            both(lambda to, second: move(place, bundle, e_own, Z, to, ZD if second else None))

        bundle_move(0)
        both(lambda to, second: move_ends(place, core, 0, to, 2 if second else None))
        for bundle in range(1, bundles):
            bundle_move(bundle)

    own_moves(lambda c: c.start())

    def onward(block, action):
        @pl.when((block < place) & (place < count - 1))
        def _():
            action(up)

        @pl.when((block > place) & (place > 0))
        def _():
            action(down)

    def arrive(block, layer):
        move(block, layer, e_own, Z, up).wait_recv()
        onward(block, lambda to: move(block, layer, e_own, Z, to).start())
        move(block, layer, e_own, X, to_x).start()
        move(block, layer, e_own, Y, to_y).start()
        move(block, layer, e_own, SA, to_c).start()

    def arrive_ends(block):
        move_ends(block, core, 0, up).wait_recv()
        onward(block, lambda to: move_ends(block, core, 0, to).start())
        move_ends(block, core, 1, to_c).start()

    def cross(block, layer):
        move(block, layer, e_x, X, to_x).wait_recv()
        move(block, layer, e_y, Y, to_y).wait_recv()

        @pl.when(core == 0)
        def _():
            move(block, layer, e_x, D, to_y).start()

        @pl.when(core == 1)
        def _():
            move(block, layer, e_y, D, to_x).start()

        move(block, layer, e_x, SX, to_c).start()
        move(block, layer, e_y, SY, to_c).start()

    def corner(block, layer):
        move(block, layer, e_d, D, to_x).wait_recv()
        move(block, layer, e_d, SD, to_c).start()

    def ready(block, layer):
        move(block, layer, m_own, SA, to_c).wait_recv()
        move(block, layer, m_x, SX, to_c).wait_recv()
        move(block, layer, m_y, SY, to_c).wait_recv()
        move(block, layer, m_d, SD, to_c).wait_recv()

    def item(step, layer, ahead):
        return step + (layer + ahead) // layers, (layer + ahead) % layers

    def exchange(step, layer):
        for ahead, action in ((1, corner), (2, cross), (4, arrive)):
            later, its_layer = item(step, layer, ahead)
            if its_layer % BUNDLE:
                continue

            @pl.when((later > 0) & (later < count))
            def _():
                block = block_at(later, place, count)
                action(block, its_layer // BUNDLE)
                if action is arrive and its_layer == 0:
                    arrive_ends(block)

    rows16 = 16
    chunks = segments // 128
    lane = lax.broadcasted_iota(jnp.int32, (128, 128), 1)
    sub = lax.broadcasted_iota(jnp.int32, (128, 128), 0)
    earlier = (sub < lane).astype(F32).astype(BF16)
    names = lax.broadcasted_iota(jnp.int32, (rows16, 128), 0)
    base = names.astype(F32) * capacity
    named = [
        (jnp.broadcast_to(block_ref[:, c * 128 : (c + 1) * 128], (rows16, 128)) == names).astype(F32)
        for c in range(chunks)
    ]
    before = jnp.dot(
        jnp.concatenate(named, axis=0).astype(BF16), earlier, preferred_element_type=F32
    )
    carry = base
    for c in range(chunks):
        ahead_of = before[c * rows16 : (c + 1) * rows16] + carry
        carry = carry + jnp.sum(named[c], axis=1, keepdims=True)
        slot_row[:, c * 128 : (c + 1) * 128] = jnp.sum(named[c] * ahead_of, axis=0, keepdims=True)
    wide[:, 0:in_width] = feat_ref[...]
    ray_of = lax.broadcasted_iota(jnp.int32, (RAYS_DEV, 128), 0)
    lane_of = lax.broadcasted_iota(jnp.int32, (RAYS_DEV, 128), 1)
    ray_tag = jnp.where(lane_of == SEGS_RAY, ray_of, 0)
    for k in range(SEGS_RAY):
        tags = jnp.where(lane_of == k, 1, ray_tag)
        wide[k * RAYS_DEV : (k + 1) * RAYS_DEV, in_width : in_width + 128] = tags.astype(F32).astype(
            BF16
        )
    dens_map[...] = jnp.zeros_like(dens_map)

    pick_tile = min(256, capacity)

    def tile_loop(body, size):
        for index in range(capacity // size):
            body(slice(index * size, (index + 1) * size), index)

    rows_first = (((0,), (0,)), ((), ()))

    def gather_in(step, block):
        def body(rows, index):
            first = (block * capacity + index * pick_tile).astype(F32)
            held = jnp.clip(slot_row[...] - first, -1.0, float(pick_tile)).astype(BF16)
            wanted = lax.broadcasted_iota(jnp.int32, (pick_tile, segments), 0).astype(F32).astype(BF16)
            same = jnp.broadcast_to(held, (pick_tile, segments)) == wanted
            pick = jnp.where(same, jnp.ones((), BF16), jnp.zeros((), BF16))
            mine = jnp.dot(pick, wide[...], preferred_element_type=F32)
            tag = mine[:, in_width : in_width + 128]
            turns[step, rows] = jnp.where(lane_tile < SEGS_RAY, tag, 0.0).astype(BF16)
            on_ray = lax.broadcasted_iota(jnp.int32, (pick_tile, RAYS_DEV), 1).astype(F32)
            rays[step, rows] = (tag[:, SEGS_RAY : SEGS_RAY + 1] == on_ray).astype(F32).astype(BF16)
            act[rows] = silu(
                jnp.dot(
                    mine[:, 0:in_width].astype(BF16),
                    ends[block, 0:in_width],
                    preferred_element_type=F32,
                ).astype(BF16)
            )

        tile_loop(body, pick_tile)

    lane_tile = lax.broadcasted_iota(jnp.int32, (pick_tile, 128), 1)

    def layer_step(block, layer):
        def body(rows, index):
            value = act[rows]
            act[rows] = value + silu(
                jnp.dot(value, hid[block, layer], preferred_element_type=F32).astype(BF16)
            )

        tile_loop(body, row_tile)

    def head_step(step, block):
        w_den = jnp.broadcast_to(ends[block, in_width + feats : in_width + feats + 1], (128, hidden))
        w_head = jnp.concatenate([ends[block, in_width : in_width + feats], w_den], axis=0)
        contract = (((1,), (1,)), ((), ()))

        def body(rows, index):
            out = lax.dot_general(act[rows], w_head, contract, preferred_element_type=F32)
            heads[step, rows] = out[:, 0:feats].astype(BF16)
            density = (0.25 * softplus(out[:, feats : feats + 128])).astype(BF16)
            dens_map[...] += lax.dot_general(
                turns[step, rows] * density, rays[step, rows], rows_first, preferred_element_type=F32
            )

        tile_loop(body, row_tile)

    def step_body(step, carry_in):
        block = block_at(step, place, count)
        for layer in range(layers):
            exchange(step, layer)

            @pl.when(step > 0)
            def _():
                if layer == 0:
                    move_ends(block, core_mate, 1, to_c).wait_recv()
                if layer % BUNDLE == 0:
                    ready(block, layer // BUNDLE)

            if layer == 0:
                gather_in(step, block)
            layer_step(block, layer)
        head_step(step, block)
        return carry_in

    lax.fori_loop(0, count, step_body, 0)

    density = dens_map[0:SEGS_RAY]
    optical = jnp.zeros((SEGS_RAY, RAYS_DEV), F32)
    for k in range(SEGS_RAY):
        nearer = rank_ref[k : k + 1, :] < rank_ref[...]
        optical += jnp.where(nearer, density[k : k + 1], 0.0)
    weight = jnp.exp(-optical) * (1.0 - jnp.exp(-density))
    weight = jnp.concatenate([weight, jnp.zeros((128 - SEGS_RAY, RAYS_DEV), F32)], axis=0)
    weight = weight.astype(BF16)

    def blend(step, color):
        spread = jnp.dot(turns[step], weight, preferred_element_type=F32).astype(BF16) * rays[step]
        return color + lax.dot_general(heads[step], spread, rows_first, preferred_element_type=F32)

    color = lax.fori_loop(0, count, blend, jnp.zeros((feats, RAYS_DEV), F32))
    around[4] = color.T.astype(BF16)

    def strip(dy, dx):
        edge = CONV_LAYERS * TW
        rows = {0: (0, RAYS_DEV), -1: (0, edge), 1: (RAYS_DEV - edge, edge)}[dy]
        mine = around.at[4, pl.ds(*rows)]
        theirs = around.at[(1 - dy) * 3 + 1 - dx, pl.ds(*rows)]
        return mine, theirs

    def edge_copy(index, dy, dx):
        mine, theirs = strip(dy, dx)
        there, exists = beside(dy, dx)
        return exists, pltpu.make_async_remote_copy(
            src_ref=mine,
            dst_ref=theirs,
            send_sem=edge_send.at[index],
            recv_sem=edge_recv.at[index],
            device_id=there,
            device_id_type=MESH,
        )

    for index, (dy, dx) in enumerate(AROUND):
        exists, copy = edge_copy(index, dy, dx)

        @pl.when(exists == 1)
        def _():
            copy.start()

    for index, (dy, dx) in enumerate(AROUND):
        _, arriving = edge_copy(index, dy, dx)
        _, from_there = beside(-dy, -dx)

        @pl.when(from_there == 1)
        def _():
            arriving.wait_recv()

        exists, copy = edge_copy(index, dy, dx)

        @pl.when(exists == 1)
        def _():
            copy.wait_send()

    for a in range(3):
        for b in range(3):
            color_ref[a * TH : (a + 1) * TH, b * TW : (b + 1) * TW] = around[a * 3 + b].reshape(
                TH, TW, feats
            )

    own_moves(lambda c: c.wait_send())

    def drain(step, carry_in):
        block = block_at(step, place, count)
        onward(block, lambda to: move_ends(block, core, 0, to).wait_send())
        move_ends(block, core, 1, to_c).wait_send()
        for layer in range(bundles):
            onward(block, lambda to, layer=layer: move(block, layer, e_own, Z, to).wait_send())
            for kind in (X, Y, D, SA, SX, SY, SD):
                move(block, layer, e_own, kind, to_c).wait_send()
        return carry_in

    lax.fori_loop(1, count, drain, 0)


def render(count, tiles_count, rows, block_ids, ranks, w_in, w_hid, w_out, w_dens):
    segments, in_width = rows.shape
    capacity = 2 * segments // count
    layers, hidden, _ = w_hid.shape
    feats = w_out.shape[1]
    row_tile = min(512, capacity)
    end_rows = in_width + feats + 32
    vmem = pl.BlockSpec(memory_space=pltpu.VMEM)
    macs = count * capacity * hidden * (in_width + layers * hidden + feats)
    return pl.pallas_call(
        functools.partial(render_kernel, count, tiles_count, capacity, row_tile),
        out_shape=jax.ShapeDtypeStruct((3 * TH, 3 * TW, feats), BF16),
        in_specs=[vmem, vmem, vmem, vmem, pl.BlockSpec(memory_space=pl.ANY), vmem, vmem],
        out_specs=vmem,
        scratch_shapes=[
            pltpu.VMEM((count, layers, hidden, hidden), BF16),
            pltpu.VMEM((count, end_rows, hidden), BF16),
            pltpu.VMEM((1, segments), F32),
            pltpu.VMEM((segments, in_width + 128), BF16),
            pltpu.VMEM((count, capacity, 128), BF16),
            pltpu.VMEM((count, capacity, RAYS_DEV), BF16),
            pltpu.VMEM((capacity, hidden), BF16),
            pltpu.VMEM((count, capacity, feats), BF16),
            pltpu.VMEM((128, RAYS_DEV), F32),
            pltpu.VMEM((9, RAYS_DEV, feats), BF16),
            pltpu.SemaphoreType.DMA((8,)),
            pltpu.SemaphoreType.DMA((8,)),
            pltpu.SemaphoreType.DMA((count, layers // BUNDLE, 9)),
            pltpu.SemaphoreType.DMA((count, layers // BUNDLE, 8)),
            pltpu.SemaphoreType.DMA((count, 3)),
            pltpu.SemaphoreType.DMA((count, 2)),
            pltpu.SemaphoreType.DMA,
        ],
        compiler_params=pltpu.CompilerParams(
            collective_id=0, has_side_effects=True, vmem_limit_bytes=56 * 1024 * 1024
        ),
        cost_estimate=pl.CostEstimate(flops=2 * macs, bytes_accessed=4 << 20, transcendentals=0),
        name="render",
    )(rows, block_ids, ranks, w_in, w_hid, w_out, w_dens)


def conv_layer(padded, kernel, out_rows, out_cols):
    pieces = []
    for offset_y in range(3):
        for offset_x in range(3):
            pieces.append(padded[offset_y : offset_y + out_rows, offset_x : offset_x + out_cols])
    patches = jnp.concatenate(pieces, axis=-1)
    channels = kernel.shape[-1]
    result = jnp.dot(
        patches, kernel.reshape(9 * kernel.shape[2], channels), preferred_element_type=jnp.float32
    )
    center = padded[1 : 1 + out_rows, 1 : 1 + out_cols].astype(jnp.float32)
    return (center + jax.nn.silu(result)).astype(jnp.bfloat16)


def shards(seg_feat, seg_block, depth_rank, w_in, w_hidden, w_out, w_dens, conv_w):
    block_count = lax.axis_size("blocks")
    segments = seg_feat.shape[2]
    color = render(
        block_count,
        lax.axis_size("tiles"),
        seg_feat[0, 0],
        seg_block.reshape(1, segments),
        depth_rank[0, 0],
        w_in[0],
        w_hidden[0],
        w_out[0],
        w_dens,
    )
    top, left = TH - CONV_LAYERS, TW - CONV_LAYERS
    tile_image = color[top : 2 * TH + CONV_LAYERS, left : 2 * TW + CONV_LAYERS]
    rows_total = TH * lax.axis_size(("tiles", "sub"))
    cols_total = TW * block_count
    row_pos = (
        lax.axis_index(("tiles", "sub")) * TH
        - CONV_LAYERS
        + jnp.arange(TH + 2 * CONV_LAYERS, dtype=jnp.int32)
    )
    col_pos = (
        lax.axis_index("blocks") * TW
        - CONV_LAYERS
        + jnp.arange(TW + 2 * CONV_LAYERS, dtype=jnp.int32)
    )
    inside = ((row_pos >= 0) & (row_pos < rows_total))[:, None] & (
        (col_pos >= 0) & (col_pos < cols_total)
    )[None, :]
    current = tile_image
    for layer_index in range(CONV_LAYERS):
        margin = CONV_LAYERS - layer_index - 1
        size_h = TH + 2 * margin
        size_w = TW + 2 * margin
        current = conv_layer(current, conv_w[layer_index], size_h, size_w)
        keep_mask = inside[
            layer_index + 1 : layer_index + 1 + size_h, layer_index + 1 : layer_index + 1 + size_w
        ]
        current = jnp.where(keep_mask[:, :, None], current, jnp.zeros_like(current))
    tile_image = current
    return tile_image


def solution(mesh):
    in_specs = (
        P(("groups", "tiles", "sub"), "blocks", None, None),
        P(("groups", "tiles", "sub"), "blocks", None, None),
        P(("groups", "tiles", "sub"), "blocks", None, None),
        P("blocks", None, None),
        P("blocks", None, None, None),
        P("blocks", None, None),
        P("blocks", None),
        P(),
    )
    out_specs = P(("groups", "tiles", "sub"), "blocks", None)
    return jax.shard_map(shards, mesh=mesh, in_specs=in_specs, out_specs=out_specs, check_vma=False)
```

```python
import functools

import jax
import jax.numpy as jnp
from jax import lax
from jax.experimental import pallas as pl
from jax.experimental.pallas import tpu as pltpu
from jax.sharding import PartitionSpec as P

SEGS_RAY = 8
CONV_LAYERS = 3
TW = 16
TH = 16
RAYS_DEV = 256
MESH = pl.DeviceIdType.MESH
F32 = jnp.float32
BF16 = jnp.bfloat16


def silu(value):
    half = value * jnp.asarray(0.5, value.dtype)
    return half + half * jnp.tanh(half)


def softplus(value):
    return jnp.maximum(value, 0.0) + jnp.log1p(jnp.exp(-jnp.abs(value)))


def block_at(step, place, count):
    near = jnp.minimum(place, count - 1 - place)
    distance = (step + 1) // 2
    paired = jnp.where(step % 2 == 1, place + distance, place - distance)
    rest = jnp.where(2 * place <= count - 1, step, count - 1 - step)
    return jnp.where(step <= 2 * near, paired, rest)


BUNDLE = 2
AROUND = [(dy, dx) for dy in (-1, 0, 1) for dx in (-1, 0, 1) if (dy, dx) != (0, 0)]
Z, X, Y, D, SA, SX, SY, SD, ZD = range(9)


def render_kernel(
    count,
    tiles_count,
    capacity,
    row_tile,
    feat_ref,
    block_ref,
    rank_ref,
    w_in_ref,
    w_hid_ref,
    w_out_ref,
    w_dens_ref,
    color_ref,
    hid,
    ends,
    slot_row,
    wide,
    turns,
    rays,
    act,
    heads,
    dens_map,
    around,
    edge_send,
    edge_recv,
    send_sem,
    recv_sem,
    ends_send,
    ends_recv,
    own_sem,
):
    place = lax.axis_index("blocks")
    tile = lax.axis_index("tiles")
    group = lax.axis_index("groups")
    core = lax.axis_index("sub")
    tile_mate = tile + 1 - 2 * (tile % 2)
    group_mate = group + 1 - 2 * (group % 2)
    core_mate = 1 - core
    tx, gy = tile % 2, group % 2
    layers = w_hid_ref.shape[0]
    hidden = w_hid_ref.shape[2]
    bundles = layers // BUNDLE
    part = hidden // 8
    end_rows = ends.shape[1]
    end_half = end_rows // 2
    feats = w_out_ref.shape[1]
    in_width = w_in_ref.shape[0]
    segments = feat_ref.shape[0]

    def eighth(a, b, c):
        return (a * 2 + b) * 2 + c

    to_x, to_y, to_c = {"tiles": tile_mate}, {"groups": group_mate}, {"sub": core_mate}

    line = tile * 2 + core
    lines = 2 * tiles_count

    def beside(dy, dx):
        row, column = line + dy, place + dx
        exists = 1
        if dy < 0:
            exists = exists * jnp.minimum(line, 1)
        if dy > 0:
            exists = exists * jnp.minimum(lines - 1 - line, 1)
        if dx < 0:
            exists = exists * jnp.minimum(place, 1)
        if dx > 0:
            exists = exists * jnp.minimum(count - 1 - place, 1)
        return {"tiles": (row + 2) // 2 - 1, "sub": (row + 2) % 2, "blocks": column}, exists

    barrier = pltpu.get_barrier_semaphore()
    pl.semaphore_signal(barrier, inc=1, device_id=to_x, device_id_type=MESH)
    pl.semaphore_signal(barrier, inc=1, device_id=to_y, device_id_type=MESH)
    pl.semaphore_signal(barrier, inc=1, device_id=to_c, device_id_type=MESH)

    @pl.when(place > 0)
    def _():
        pl.semaphore_signal(barrier, inc=1, device_id={"blocks": place - 1}, device_id_type=MESH)

    @pl.when(place < count - 1)
    def _():
        pl.semaphore_signal(barrier, inc=1, device_id={"blocks": place + 1}, device_id_type=MESH)

    around[...] = jnp.zeros_like(around)
    own = pltpu.make_async_copy(w_hid_ref, hid.at[place], own_sem)
    own.start()
    ends[place, 0:in_width] = w_in_ref[...]
    ends[place, in_width : in_width + feats] = w_out_ref[...].T
    ends[place, in_width + feats : end_rows] = jnp.broadcast_to(
        w_dens_ref[...], (end_rows - in_width - feats, hidden)
    )
    own.wait()

    peers = 3 + jnp.minimum(place, 1) + jnp.minimum(count - 1 - place, 1)
    for dy, dx in AROUND:
        there, exists = beside(dy, dx)

        @pl.when(exists == 1)
        def _():
            pl.semaphore_signal(barrier, inc=1, device_id=there, device_id_type=MESH)

        peers = peers + exists
    pl.semaphore_wait(barrier, peers)

    def piece(block, layer, which):
        return hid.at[
            block, pl.ds(layer * BUNDLE, BUNDLE), pl.ds(pl.multiple_of(which * part, part), part)
        ]

    def move(block, layer, which, kind, target, send_kind=None):
        ref = piece(block, layer, which)
        return pltpu.make_async_remote_copy(
            src_ref=ref,
            dst_ref=ref,
            send_sem=send_sem.at[block, layer, kind if send_kind is None else send_kind],
            recv_sem=recv_sem.at[block, layer, kind],
            device_id=target,
            device_id_type=MESH,
        )

    def move_ends(block, half, kind, target, send_kind=None):
        ref = ends.at[block, pl.ds(pl.multiple_of(half * end_half, end_half), end_half)]
        return pltpu.make_async_remote_copy(
            src_ref=ref,
            dst_ref=ref,
            send_sem=ends_send.at[block, kind if send_kind is None else send_kind],
            recv_sem=ends_recv.at[block, kind],
            device_id=target,
            device_id_type=MESH,
        )

    e_own = eighth(tx, gy, core)
    e_x = eighth(1 - tx, gy, core)
    e_y = eighth(tx, 1 - gy, core)
    e_d = eighth(1 - tx, 1 - gy, core)
    m_own = eighth(tx, gy, core_mate)
    m_x = eighth(1 - tx, gy, core_mate)
    m_y = eighth(tx, 1 - gy, core_mate)
    m_d = eighth(1 - tx, 1 - gy, core_mate)
    up, down = {"blocks": place + 1}, {"blocks": place - 1}

    def own_moves(action):
        def both(make):
            @pl.when(place < count - 1)
            def _():
                action(make(up, None))

            @pl.when(place > 0)
            def _():
                action(make(down, True))

        def bundle_move(bundle):
            both(lambda to, second: move(place, bundle, e_own, Z, to, ZD if second else None))

        bundle_move(0)
        both(lambda to, second: move_ends(place, core, 0, to, 2 if second else None))
        for bundle in range(1, bundles):
            bundle_move(bundle)

    own_moves(lambda c: c.start())

    def onward(block, action):
        @pl.when((block < place) & (place < count - 1))
        def _():
            action(up)

        @pl.when((block > place) & (place > 0))
        def _():
            action(down)

    def arrive(block, layer):
        move(block, layer, e_own, Z, up).wait_recv()
        onward(block, lambda to: move(block, layer, e_own, Z, to).start())
        move(block, layer, e_own, X, to_x).start()
        move(block, layer, e_own, Y, to_y).start()
        move(block, layer, e_own, SA, to_c).start()

    def arrive_ends(block):
        move_ends(block, core, 0, up).wait_recv()
        onward(block, lambda to: move_ends(block, core, 0, to).start())
        move_ends(block, core, 1, to_c).start()

    def cross(block, layer):
        move(block, layer, e_x, X, to_x).wait_recv()
        move(block, layer, e_y, Y, to_y).wait_recv()

        @pl.when(core == 0)
        def _():
            move(block, layer, e_x, D, to_y).start()

        @pl.when(core == 1)
        def _():
            move(block, layer, e_y, D, to_x).start()

        move(block, layer, e_x, SX, to_c).start()
        move(block, layer, e_y, SY, to_c).start()

    def corner(block, layer):
        move(block, layer, e_d, D, to_x).wait_recv()
        move(block, layer, e_d, SD, to_c).start()

    def ready(block, layer):
        move(block, layer, m_own, SA, to_c).wait_recv()
        move(block, layer, m_x, SX, to_c).wait_recv()
        move(block, layer, m_y, SY, to_c).wait_recv()
        move(block, layer, m_d, SD, to_c).wait_recv()

    def item(step, layer, ahead):
        return step + (layer + ahead) // layers, (layer + ahead) % layers

    def exchange(step, layer):
        for ahead, action in ((1, corner), (2, cross), (4, arrive)):
            later, its_layer = item(step, layer, ahead)
            if its_layer % BUNDLE:
                continue

            @pl.when((later > 0) & (later < count))
            def _():
                block = block_at(later, place, count)
                action(block, its_layer // BUNDLE)
                if action is arrive and its_layer == 0:
                    arrive_ends(block)

    rows16 = 16
    chunks = segments // 128
    lane = lax.broadcasted_iota(jnp.int32, (128, 128), 1)
    sub = lax.broadcasted_iota(jnp.int32, (128, 128), 0)
    earlier = (sub < lane).astype(F32).astype(BF16)
    names = lax.broadcasted_iota(jnp.int32, (rows16, 128), 0)
    base = names.astype(F32) * capacity
    named = [
        (jnp.broadcast_to(block_ref[:, c * 128 : (c + 1) * 128], (rows16, 128)) == names).astype(F32)
        for c in range(chunks)
    ]
    before = jnp.dot(
        jnp.concatenate(named, axis=0).astype(BF16), earlier, preferred_element_type=F32
    )
    carry = base
    for c in range(chunks):
        ahead_of = before[c * rows16 : (c + 1) * rows16] + carry
        carry = carry + jnp.sum(named[c], axis=1, keepdims=True)
        slot_row[:, c * 128 : (c + 1) * 128] = jnp.sum(named[c] * ahead_of, axis=0, keepdims=True)
    wide[:, 0:in_width] = feat_ref[...]
    ray_of = lax.broadcasted_iota(jnp.int32, (RAYS_DEV, 128), 0)
    lane_of = lax.broadcasted_iota(jnp.int32, (RAYS_DEV, 128), 1)
    ray_tag = jnp.where(lane_of == SEGS_RAY, ray_of, 0)
    for k in range(SEGS_RAY):
        tags = jnp.where(lane_of == k, 1, ray_tag)
        wide[k * RAYS_DEV : (k + 1) * RAYS_DEV, in_width : in_width + 128] = tags.astype(F32).astype(
            BF16
        )
    dens_map[...] = jnp.zeros_like(dens_map)

    pick_tile = min(256, capacity)

    def tile_loop(body, size):
        for index in range(capacity // size):
            body(slice(index * size, (index + 1) * size), index)

    rows_first = (((0,), (0,)), ((), ()))

    def gather_in(step, block):
        def body(rows, index):
            first = (block * capacity + index * pick_tile).astype(F32)
            held = jnp.clip(slot_row[...] - first, -1.0, float(pick_tile)).astype(BF16)
            wanted = lax.broadcasted_iota(jnp.int32, (pick_tile, segments), 0).astype(F32).astype(BF16)
            same = jnp.broadcast_to(held, (pick_tile, segments)) == wanted
            pick = jnp.where(same, jnp.ones((), BF16), jnp.zeros((), BF16))
            mine = jnp.dot(pick, wide[...], preferred_element_type=F32)
            tag = mine[:, in_width : in_width + 128]
            turns[step, rows] = jnp.where(lane_tile < SEGS_RAY, tag, 0.0).astype(BF16)
            on_ray = lax.broadcasted_iota(jnp.int32, (pick_tile, RAYS_DEV), 1).astype(F32)
            rays[step, rows] = (tag[:, SEGS_RAY : SEGS_RAY + 1] == on_ray).astype(F32).astype(BF16)
            act[rows] = silu(
                jnp.dot(
                    mine[:, 0:in_width].astype(BF16),
                    ends[block, 0:in_width],
                    preferred_element_type=F32,
                ).astype(BF16)
            )

        tile_loop(body, pick_tile)

    lane_tile = lax.broadcasted_iota(jnp.int32, (pick_tile, 128), 1)

    def layer_step(block, layer):
        def body(rows, index):
            value = act[rows]
            act[rows] = value + silu(
                jnp.dot(value, hid[block, layer], preferred_element_type=F32).astype(BF16)
            )

        tile_loop(body, row_tile)

    def head_step(step, block):
        w_den = jnp.broadcast_to(ends[block, in_width + feats : in_width + feats + 1], (128, hidden))
        w_head = jnp.concatenate([ends[block, in_width : in_width + feats], w_den], axis=0)
        contract = (((1,), (1,)), ((), ()))

        def body(rows, index):
            out = lax.dot_general(act[rows], w_head, contract, preferred_element_type=F32)
            heads[step, rows] = out[:, 0:feats].astype(BF16)
            density = (0.25 * softplus(out[:, feats : feats + 128])).astype(BF16)
            dens_map[...] += lax.dot_general(
                turns[step, rows] * density, rays[step, rows], rows_first, preferred_element_type=F32
            )

        tile_loop(body, row_tile)

    def step_body(step, carry_in):
        block = block_at(step, place, count)
        for layer in range(layers):
            exchange(step, layer)

            @pl.when(step > 0)
            def _():
                if layer == 0:
                    move_ends(block, core_mate, 1, to_c).wait_recv()
                if layer % BUNDLE == 0:
                    ready(block, layer // BUNDLE)

            if layer == 0:
                gather_in(step, block)
            layer_step(block, layer)
        head_step(step, block)
        return carry_in

    lax.fori_loop(0, count, step_body, 0)

    density = dens_map[0:SEGS_RAY]
    optical = jnp.zeros((SEGS_RAY, RAYS_DEV), F32)
    for k in range(SEGS_RAY):
        nearer = rank_ref[k : k + 1, :] < rank_ref[...]
        optical += jnp.where(nearer, density[k : k + 1], 0.0)
    weight = jnp.exp(-optical) * (1.0 - jnp.exp(-density))
    weight = jnp.concatenate([weight, jnp.zeros((128 - SEGS_RAY, RAYS_DEV), F32)], axis=0)
    weight = weight.astype(BF16)

    def blend(step, color):
        spread = jnp.dot(turns[step], weight, preferred_element_type=F32).astype(BF16) * rays[step]
        return color + lax.dot_general(heads[step], spread, rows_first, preferred_element_type=F32)

    color = lax.fori_loop(0, count, blend, jnp.zeros((feats, RAYS_DEV), F32))
    around[4] = color.T.astype(BF16)

    def strip(dy, dx):
        edge = CONV_LAYERS * TW
        rows = {0: (0, RAYS_DEV), -1: (0, edge), 1: (RAYS_DEV - edge, edge)}[dy]
        mine = around.at[4, pl.ds(*rows)]
        theirs = around.at[(1 - dy) * 3 + 1 - dx, pl.ds(*rows)]
        return mine, theirs

    def edge_copy(index, dy, dx):
        mine, theirs = strip(dy, dx)
        there, exists = beside(dy, dx)
        return exists, pltpu.make_async_remote_copy(
            src_ref=mine,
            dst_ref=theirs,
            send_sem=edge_send.at[index],
            recv_sem=edge_recv.at[index],
            device_id=there,
            device_id_type=MESH,
        )

    for index, (dy, dx) in enumerate(AROUND):
        exists, copy = edge_copy(index, dy, dx)

        @pl.when(exists == 1)
        def _():
            copy.start()

    for index, (dy, dx) in enumerate(AROUND):
        _, arriving = edge_copy(index, dy, dx)
        _, from_there = beside(-dy, -dx)

        @pl.when(from_there == 1)
        def _():
            arriving.wait_recv()

        exists, copy = edge_copy(index, dy, dx)

        @pl.when(exists == 1)
        def _():
            copy.wait_send()

    for a in range(3):
        for b in range(3):
            color_ref[a * TH : (a + 1) * TH, b * TW : (b + 1) * TW] = around[a * 3 + b].reshape(
                TH, TW, feats
            )

    own_moves(lambda c: c.wait_send())

    def drain(step, carry_in):
        block = block_at(step, place, count)
        onward(block, lambda to: move_ends(block, core, 0, to).wait_send())
        move_ends(block, core, 1, to_c).wait_send()
        for layer in range(bundles):
            onward(block, lambda to, layer=layer: move(block, layer, e_own, Z, to).wait_send())
            for kind in (X, Y, D, SA, SX, SY, SD):
                move(block, layer, e_own, kind, to_c).wait_send()
        return carry_in

    lax.fori_loop(1, count, drain, 0)


def render(count, tiles_count, rows, block_ids, ranks, w_in, w_hid, w_out, w_dens):
    segments, in_width = rows.shape
    capacity = 2 * segments // count
    layers, hidden, _ = w_hid.shape
    feats = w_out.shape[1]
    row_tile = min(512, capacity)
    end_rows = in_width + feats + 32
    vmem = pl.BlockSpec(memory_space=pltpu.VMEM)
    macs = count * capacity * hidden * (in_width + layers * hidden + feats)
    return pl.pallas_call(
        functools.partial(render_kernel, count, tiles_count, capacity, row_tile),
        out_shape=jax.ShapeDtypeStruct((3 * TH, 3 * TW, feats), BF16),
        in_specs=[vmem, vmem, vmem, vmem, pl.BlockSpec(memory_space=pl.ANY), vmem, vmem],
        out_specs=vmem,
        scratch_shapes=[
            pltpu.VMEM((count, layers, hidden, hidden), BF16),
            pltpu.VMEM((count, end_rows, hidden), BF16),
            pltpu.VMEM((1, segments), F32),
            pltpu.VMEM((segments, in_width + 128), BF16),
            pltpu.VMEM((count, capacity, 128), BF16),
            pltpu.VMEM((count, capacity, RAYS_DEV), BF16),
            pltpu.VMEM((capacity, hidden), BF16),
            pltpu.VMEM((count, capacity, feats), BF16),
            pltpu.VMEM((128, RAYS_DEV), F32),
            pltpu.VMEM((9, RAYS_DEV, feats), BF16),
            pltpu.SemaphoreType.DMA((8,)),
            pltpu.SemaphoreType.DMA((8,)),
            pltpu.SemaphoreType.DMA((count, layers // BUNDLE, 9)),
            pltpu.SemaphoreType.DMA((count, layers // BUNDLE, 8)),
            pltpu.SemaphoreType.DMA((count, 3)),
            pltpu.SemaphoreType.DMA((count, 2)),
            pltpu.SemaphoreType.DMA,
        ],
        compiler_params=pltpu.CompilerParams(
            collective_id=0, has_side_effects=True, vmem_limit_bytes=56 * 1024 * 1024
        ),
        cost_estimate=pl.CostEstimate(flops=2 * macs, bytes_accessed=4 << 20, transcendentals=0),
        name="render",
    )(rows, block_ids, ranks, w_in, w_hid, w_out, w_dens)


def conv_layer(padded, kernel, out_rows, out_cols):
    pieces = []
    for offset_y in range(3):
        for offset_x in range(3):
            pieces.append(padded[offset_y : offset_y + out_rows, offset_x : offset_x + out_cols])
    patches = jnp.concatenate(pieces, axis=-1)
    channels = kernel.shape[-1]
    result = jnp.dot(
        patches, kernel.reshape(9 * kernel.shape[2], channels), preferred_element_type=jnp.float32
    )
    center = padded[1 : 1 + out_rows, 1 : 1 + out_cols].astype(jnp.float32)
    return (center + jax.nn.silu(result)).astype(jnp.bfloat16)


def shards(seg_feat, seg_block, depth_rank, w_in, w_hidden, w_out, w_dens, conv_w):
    block_count = lax.axis_size("blocks")
    segments = seg_feat.shape[2]
    color = render(
        block_count,
        lax.axis_size("tiles"),
        seg_feat[0, 0],
        seg_block.reshape(1, segments),
        depth_rank[0, 0],
        w_in[0],
        w_hidden[0],
        w_out[0],
        w_dens,
    )
    top, left = TH - CONV_LAYERS, TW - CONV_LAYERS
    tile_image = lax.optimization_barrier(
        color[top : 2 * TH + CONV_LAYERS, left : 2 * TW + CONV_LAYERS]
    )
    rows_total = TH * lax.axis_size(("tiles", "sub"))
    cols_total = TW * block_count
    row_pos = (
        lax.axis_index(("tiles", "sub")) * TH
        - CONV_LAYERS
        + jnp.arange(TH + 2 * CONV_LAYERS, dtype=jnp.int32)
    )
    col_pos = (
        lax.axis_index("blocks") * TW
        - CONV_LAYERS
        + jnp.arange(TW + 2 * CONV_LAYERS, dtype=jnp.int32)
    )
    inside = ((row_pos >= 0) & (row_pos < rows_total))[:, None] & (
        (col_pos >= 0) & (col_pos < cols_total)
    )[None, :]
    current = tile_image
    for layer_index in range(CONV_LAYERS):
        margin = CONV_LAYERS - layer_index - 1
        size_h = TH + 2 * margin
        size_w = TW + 2 * margin
        current = conv_layer(current, conv_w[layer_index], size_h, size_w)
        keep_mask = inside[
            layer_index + 1 : layer_index + 1 + size_h, layer_index + 1 : layer_index + 1 + size_w
        ]
        current = jnp.where(keep_mask[:, :, None], current, jnp.zeros_like(current))
    tile_image = current
    return tile_image


def solution(mesh):
    in_specs = (
        P(("groups", "tiles", "sub"), "blocks", None, None),
        P(("groups", "tiles", "sub"), "blocks", None, None),
        P(("groups", "tiles", "sub"), "blocks", None, None),
        P("blocks", None, None),
        P("blocks", None, None, None),
        P("blocks", None, None),
        P("blocks", None),
        P(),
    )
    out_specs = P(("groups", "tiles", "sub"), "blocks", None)
    return jax.shard_map(shards, mesh=mesh, in_specs=in_specs, out_specs=out_specs, check_vma=False)
```

```python
import functools

import jax
import jax.numpy as jnp
from jax import lax
from jax.experimental import pallas as pl
from jax.experimental.pallas import tpu as pltpu
from jax.sharding import PartitionSpec as P

SEGS_RAY = 8
CONV_LAYERS = 3
TW = 16
TH = 16
RAYS_DEV = 256
MESH = pl.DeviceIdType.MESH
F32 = jnp.float32
BF16 = jnp.bfloat16


def silu(value):
    half = value * jnp.asarray(0.5, value.dtype)
    return half + half * jnp.tanh(half)


def softplus(value):
    return jnp.maximum(value, 0.0) + jnp.log1p(jnp.exp(-jnp.abs(value)))


def block_at(step, place, count):
    near = jnp.minimum(place, count - 1 - place)
    distance = (step + 1) // 2
    paired = jnp.where(step % 2 == 1, place + distance, place - distance)
    rest = jnp.where(2 * place <= count - 1, step, count - 1 - step)
    return jnp.where(step <= 2 * near, paired, rest)


BUNDLE = 2
AROUND = [(dy, dx) for dy in (-1, 0, 1) for dx in (-1, 0, 1) if (dy, dx) != (0, 0)]
Z, X, Y, D, SA, SX, SY, SD, ZD = range(9)


def render_kernel(
    count,
    tiles_count,
    capacity,
    row_tile,
    feat_ref,
    block_ref,
    rank_ref,
    w_in_ref,
    w_hid_ref,
    w_out_ref,
    w_dens_ref,
    color_ref,
    hid,
    ends,
    slot_row,
    wide,
    turns,
    rays,
    act,
    heads,
    dens_map,
    around,
    edge_send,
    edge_recv,
    send_sem,
    recv_sem,
    ends_send,
    ends_recv,
    own_sem,
):
    place = lax.axis_index("blocks")
    tile = lax.axis_index("tiles")
    group = lax.axis_index("groups")
    core = lax.axis_index("sub")
    tile_mate = tile + 1 - 2 * (tile % 2)
    group_mate = group + 1 - 2 * (group % 2)
    core_mate = 1 - core
    tx, gy = tile % 2, group % 2
    layers = w_hid_ref.shape[0]
    hidden = w_hid_ref.shape[2]
    bundles = layers // BUNDLE
    part = hidden // 8
    end_rows = ends.shape[1]
    end_half = end_rows // 2
    feats = w_out_ref.shape[1]
    in_width = w_in_ref.shape[0]
    segments = feat_ref.shape[0]

    def eighth(a, b, c):
        return (a * 2 + b) * 2 + c

    to_x, to_y, to_c = {"tiles": tile_mate}, {"groups": group_mate}, {"sub": core_mate}

    line = tile * 2 + core
    lines = 2 * tiles_count

    def beside(dy, dx):
        row, column = line + dy, place + dx
        exists = 1
        if dy < 0:
            exists = exists * jnp.minimum(line, 1)
        if dy > 0:
            exists = exists * jnp.minimum(lines - 1 - line, 1)
        if dx < 0:
            exists = exists * jnp.minimum(place, 1)
        if dx > 0:
            exists = exists * jnp.minimum(count - 1 - place, 1)
        return {"tiles": (row + 2) // 2 - 1, "sub": (row + 2) % 2, "blocks": column}, exists

    barrier = pltpu.get_barrier_semaphore()
    pl.semaphore_signal(barrier, inc=1, device_id=to_x, device_id_type=MESH)
    pl.semaphore_signal(barrier, inc=1, device_id=to_y, device_id_type=MESH)
    pl.semaphore_signal(barrier, inc=1, device_id=to_c, device_id_type=MESH)

    @pl.when(place > 0)
    def _():
        pl.semaphore_signal(barrier, inc=1, device_id={"blocks": place - 1}, device_id_type=MESH)

    @pl.when(place < count - 1)
    def _():
        pl.semaphore_signal(barrier, inc=1, device_id={"blocks": place + 1}, device_id_type=MESH)

    around[...] = jnp.zeros_like(around)
    own = pltpu.make_async_copy(w_hid_ref, hid.at[place], own_sem)
    own.start()
    ends[place, 0:in_width] = w_in_ref[...]
    ends[place, in_width : in_width + feats] = w_out_ref[...].T
    ends[place, in_width + feats : end_rows] = jnp.broadcast_to(
        w_dens_ref[...], (end_rows - in_width - feats, hidden)
    )
    own.wait()

    peers = 3 + jnp.minimum(place, 1) + jnp.minimum(count - 1 - place, 1)
    for dy, dx in AROUND:
        there, exists = beside(dy, dx)

        @pl.when(exists == 1)
        def _():
            pl.semaphore_signal(barrier, inc=1, device_id=there, device_id_type=MESH)

        peers = peers + exists
    pl.semaphore_wait(barrier, peers)

    def piece(block, layer, which):
        return hid.at[
            block, pl.ds(layer * BUNDLE, BUNDLE), pl.ds(pl.multiple_of(which * part, part), part)
        ]

    def move(block, layer, which, kind, target, send_kind=None):
        ref = piece(block, layer, which)
        return pltpu.make_async_remote_copy(
            src_ref=ref,
            dst_ref=ref,
            send_sem=send_sem.at[block, layer, kind if send_kind is None else send_kind],
            recv_sem=recv_sem.at[block, layer, kind],
            device_id=target,
            device_id_type=MESH,
        )

    def move_ends(block, half, kind, target, send_kind=None):
        ref = ends.at[block, pl.ds(pl.multiple_of(half * end_half, end_half), end_half)]
        return pltpu.make_async_remote_copy(
            src_ref=ref,
            dst_ref=ref,
            send_sem=ends_send.at[block, kind if send_kind is None else send_kind],
            recv_sem=ends_recv.at[block, kind],
            device_id=target,
            device_id_type=MESH,
        )

    e_own = eighth(tx, gy, core)
    e_x = eighth(1 - tx, gy, core)
    e_y = eighth(tx, 1 - gy, core)
    e_d = eighth(1 - tx, 1 - gy, core)
    m_own = eighth(tx, gy, core_mate)
    m_x = eighth(1 - tx, gy, core_mate)
    m_y = eighth(tx, 1 - gy, core_mate)
    m_d = eighth(1 - tx, 1 - gy, core_mate)
    up, down = {"blocks": place + 1}, {"blocks": place - 1}

    def own_moves(action):
        def both(make):
            @pl.when(place < count - 1)
            def _():
                action(make(up, None))

            @pl.when(place > 0)
            def _():
                action(make(down, True))

        def bundle_move(bundle):
            both(lambda to, second: move(place, bundle, e_own, Z, to, ZD if second else None))

        bundle_move(0)
        both(lambda to, second: move_ends(place, core, 0, to, 2 if second else None))
        for bundle in range(1, bundles):
            bundle_move(bundle)

    own_moves(lambda c: c.start())

    def onward(block, action):
        @pl.when((block < place) & (place < count - 1))
        def _():
            action(up)

        @pl.when((block > place) & (place > 0))
        def _():
            action(down)

    def arrive(block, layer):
        move(block, layer, e_own, Z, up).wait_recv()
        onward(block, lambda to: move(block, layer, e_own, Z, to).start())
        move(block, layer, e_own, X, to_x).start()
        move(block, layer, e_own, Y, to_y).start()
        move(block, layer, e_own, SA, to_c).start()

    def arrive_ends(block):
        move_ends(block, core, 0, up).wait_recv()
        onward(block, lambda to: move_ends(block, core, 0, to).start())
        move_ends(block, core, 1, to_c).start()

    def cross(block, layer):
        move(block, layer, e_x, X, to_x).wait_recv()
        move(block, layer, e_y, Y, to_y).wait_recv()

        @pl.when(core == 0)
        def _():
            move(block, layer, e_x, D, to_y).start()

        @pl.when(core == 1)
        def _():
            move(block, layer, e_y, D, to_x).start()

        move(block, layer, e_x, SX, to_c).start()
        move(block, layer, e_y, SY, to_c).start()

    def corner(block, layer):
        move(block, layer, e_d, D, to_x).wait_recv()
        move(block, layer, e_d, SD, to_c).start()

    def ready(block, layer):
        move(block, layer, m_own, SA, to_c).wait_recv()
        move(block, layer, m_x, SX, to_c).wait_recv()
        move(block, layer, m_y, SY, to_c).wait_recv()
        move(block, layer, m_d, SD, to_c).wait_recv()

    def item(step, layer, ahead):
        return step + (layer + ahead) // layers, (layer + ahead) % layers

    def exchange(step, layer):
        for ahead, action in ((3, corner), (4, cross), (6, arrive)):
            later, its_layer = item(step, layer, ahead)
            if its_layer % BUNDLE:
                continue

            @pl.when((later > 0) & (later < count))
            def _():
                block = block_at(later, place, count)
                action(block, its_layer // BUNDLE)
                if action is arrive and its_layer == 0:
                    arrive_ends(block)

    rows16 = 16
    chunks = segments // 128
    lane = lax.broadcasted_iota(jnp.int32, (128, 128), 1)
    sub = lax.broadcasted_iota(jnp.int32, (128, 128), 0)
    earlier = (sub < lane).astype(F32).astype(BF16)
    names = lax.broadcasted_iota(jnp.int32, (rows16, 128), 0)
    base = names.astype(F32) * capacity
    named = [
        (jnp.broadcast_to(block_ref[:, c * 128 : (c + 1) * 128], (rows16, 128)) == names).astype(F32)
        for c in range(chunks)
    ]
    before = jnp.dot(
        jnp.concatenate(named, axis=0).astype(BF16), earlier, preferred_element_type=F32
    )
    carry = base
    for c in range(chunks):
        ahead_of = before[c * rows16 : (c + 1) * rows16] + carry
        carry = carry + jnp.sum(named[c], axis=1, keepdims=True)
        slot_row[:, c * 128 : (c + 1) * 128] = jnp.sum(named[c] * ahead_of, axis=0, keepdims=True)
    wide[:, 0:in_width] = feat_ref[...]
    ray_of = lax.broadcasted_iota(jnp.int32, (RAYS_DEV, 128), 0)
    lane_of = lax.broadcasted_iota(jnp.int32, (RAYS_DEV, 128), 1)
    ray_tag = jnp.where(lane_of == SEGS_RAY, ray_of, 0)
    for k in range(SEGS_RAY):
        tags = jnp.where(lane_of == k, 1, ray_tag)
        wide[k * RAYS_DEV : (k + 1) * RAYS_DEV, in_width : in_width + 128] = tags.astype(F32).astype(
            BF16
        )
    dens_map[...] = jnp.zeros_like(dens_map)

    pick_tile = min(256, capacity)

    def tile_loop(body, size):
        for index in range(capacity // size):
            body(slice(index * size, (index + 1) * size), index)

    rows_first = (((0,), (0,)), ((), ()))

    def gather_in(step, block):
        def body(rows, index):
            first = (block * capacity + index * pick_tile).astype(F32)
            held = jnp.clip(slot_row[...] - first, -1.0, float(pick_tile)).astype(BF16)
            wanted = lax.broadcasted_iota(jnp.int32, (pick_tile, segments), 0).astype(F32).astype(BF16)
            same = jnp.broadcast_to(held, (pick_tile, segments)) == wanted
            pick = jnp.where(same, jnp.ones((), BF16), jnp.zeros((), BF16))
            mine = jnp.dot(pick, wide[...], preferred_element_type=F32)
            tag = mine[:, in_width : in_width + 128]
            turns[step, rows] = jnp.where(lane_tile < SEGS_RAY, tag, 0.0).astype(BF16)
            on_ray = lax.broadcasted_iota(jnp.int32, (pick_tile, RAYS_DEV), 1).astype(F32)
            rays[step, rows] = (tag[:, SEGS_RAY : SEGS_RAY + 1] == on_ray).astype(F32).astype(BF16)
            act[rows] = silu(
                jnp.dot(
                    mine[:, 0:in_width].astype(BF16),
                    ends[block, 0:in_width],
                    preferred_element_type=F32,
                ).astype(BF16)
            )

        tile_loop(body, pick_tile)

    lane_tile = lax.broadcasted_iota(jnp.int32, (pick_tile, 128), 1)

    def layer_step(block, layer):
        def body(rows, index):
            value = act[rows]
            act[rows] = value + silu(
                jnp.dot(value, hid[block, layer], preferred_element_type=F32).astype(BF16)
            )

        tile_loop(body, row_tile)

    def head_step(step, block):
        w_den = jnp.broadcast_to(ends[block, in_width + feats : in_width + feats + 1], (128, hidden))
        w_head = jnp.concatenate([ends[block, in_width : in_width + feats], w_den], axis=0)
        contract = (((1,), (1,)), ((), ()))

        def body(rows, index):
            out = lax.dot_general(act[rows], w_head, contract, preferred_element_type=F32)
            heads[step, rows] = out[:, 0:feats].astype(BF16)
            density = (0.25 * softplus(out[:, feats : feats + 128])).astype(BF16)
            dens_map[...] += lax.dot_general(
                turns[step, rows] * density, rays[step, rows], rows_first, preferred_element_type=F32
            )

        tile_loop(body, row_tile)

    def step_body(step, carry_in):
        block = block_at(step, place, count)
        for layer in range(layers):
            exchange(step, layer)

            @pl.when(step > 0)
            def _():
                if layer == 0:
                    move_ends(block, core_mate, 1, to_c).wait_recv()
                if layer % BUNDLE == 0:
                    ready(block, layer // BUNDLE)

            if layer == 0:
                gather_in(step, block)
            layer_step(block, layer)
        head_step(step, block)
        return carry_in

    next_block = block_at(1, place, count)
    arrive(next_block, 0)
    arrive_ends(next_block)
    lax.fori_loop(0, count, step_body, 0)

    density = dens_map[0:SEGS_RAY]
    optical = jnp.zeros((SEGS_RAY, RAYS_DEV), F32)
    for k in range(SEGS_RAY):
        nearer = rank_ref[k : k + 1, :] < rank_ref[...]
        optical += jnp.where(nearer, density[k : k + 1], 0.0)
    weight = jnp.exp(-optical) * (1.0 - jnp.exp(-density))
    weight = jnp.concatenate([weight, jnp.zeros((128 - SEGS_RAY, RAYS_DEV), F32)], axis=0)
    weight = weight.astype(BF16)

    def blend(step, color):
        spread = jnp.dot(turns[step], weight, preferred_element_type=F32).astype(BF16) * rays[step]
        return color + lax.dot_general(heads[step], spread, rows_first, preferred_element_type=F32)

    color = lax.fori_loop(0, count, blend, jnp.zeros((feats, RAYS_DEV), F32))
    around[4] = color.T.astype(BF16)

    def strip(dy, dx):
        edge = CONV_LAYERS * TW
        rows = {0: (0, RAYS_DEV), -1: (0, edge), 1: (RAYS_DEV - edge, edge)}[dy]
        mine = around.at[4, pl.ds(*rows)]
        theirs = around.at[(1 - dy) * 3 + 1 - dx, pl.ds(*rows)]
        return mine, theirs

    def edge_copy(index, dy, dx):
        mine, theirs = strip(dy, dx)
        there, exists = beside(dy, dx)
        return exists, pltpu.make_async_remote_copy(
            src_ref=mine,
            dst_ref=theirs,
            send_sem=edge_send.at[index],
            recv_sem=edge_recv.at[index],
            device_id=there,
            device_id_type=MESH,
        )

    for index, (dy, dx) in enumerate(AROUND):
        exists, copy = edge_copy(index, dy, dx)

        @pl.when(exists == 1)
        def _():
            copy.start()

    for index, (dy, dx) in enumerate(AROUND):
        _, arriving = edge_copy(index, dy, dx)
        _, from_there = beside(-dy, -dx)

        @pl.when(from_there == 1)
        def _():
            arriving.wait_recv()

        exists, copy = edge_copy(index, dy, dx)

        @pl.when(exists == 1)
        def _():
            copy.wait_send()

    for a in range(3):
        for b in range(3):
            color_ref[a * TH : (a + 1) * TH, b * TW : (b + 1) * TW] = around[a * 3 + b].reshape(
                TH, TW, feats
            )

    own_moves(lambda c: c.wait_send())

    def drain(step, carry_in):
        block = block_at(step, place, count)
        onward(block, lambda to: move_ends(block, core, 0, to).wait_send())
        move_ends(block, core, 1, to_c).wait_send()
        for layer in range(bundles):
            onward(block, lambda to, layer=layer: move(block, layer, e_own, Z, to).wait_send())
            for kind in (X, Y, D, SA, SX, SY, SD):
                move(block, layer, e_own, kind, to_c).wait_send()
        return carry_in

    lax.fori_loop(1, count, drain, 0)


def render(count, tiles_count, rows, block_ids, ranks, w_in, w_hid, w_out, w_dens):
    segments, in_width = rows.shape
    capacity = 2 * segments // count
    layers, hidden, _ = w_hid.shape
    feats = w_out.shape[1]
    row_tile = min(512, capacity)
    end_rows = in_width + feats + 32
    vmem = pl.BlockSpec(memory_space=pltpu.VMEM)
    macs = count * capacity * hidden * (in_width + layers * hidden + feats)
    return pl.pallas_call(
        functools.partial(render_kernel, count, tiles_count, capacity, row_tile),
        out_shape=jax.ShapeDtypeStruct((3 * TH, 3 * TW, feats), BF16),
        in_specs=[vmem, vmem, vmem, vmem, pl.BlockSpec(memory_space=pl.ANY), vmem, vmem],
        out_specs=vmem,
        scratch_shapes=[
            pltpu.VMEM((count, layers, hidden, hidden), BF16),
            pltpu.VMEM((count, end_rows, hidden), BF16),
            pltpu.VMEM((1, segments), F32),
            pltpu.VMEM((segments, in_width + 128), BF16),
            pltpu.VMEM((count, capacity, 128), BF16),
            pltpu.VMEM((count, capacity, RAYS_DEV), BF16),
            pltpu.VMEM((capacity, hidden), BF16),
            pltpu.VMEM((count, capacity, feats), BF16),
            pltpu.VMEM((128, RAYS_DEV), F32),
            pltpu.VMEM((9, RAYS_DEV, feats), BF16),
            pltpu.SemaphoreType.DMA((8,)),
            pltpu.SemaphoreType.DMA((8,)),
            pltpu.SemaphoreType.DMA((count, layers // BUNDLE, 9)),
            pltpu.SemaphoreType.DMA((count, layers // BUNDLE, 8)),
            pltpu.SemaphoreType.DMA((count, 3)),
            pltpu.SemaphoreType.DMA((count, 2)),
            pltpu.SemaphoreType.DMA,
        ],
        compiler_params=pltpu.CompilerParams(
            collective_id=0, has_side_effects=True, vmem_limit_bytes=56 * 1024 * 1024
        ),
        cost_estimate=pl.CostEstimate(flops=2 * macs, bytes_accessed=4 << 20, transcendentals=0),
        name="render",
    )(rows, block_ids, ranks, w_in, w_hid, w_out, w_dens)


def conv_layer(padded, kernel, out_rows, out_cols):
    pieces = []
    for offset_y in range(3):
        for offset_x in range(3):
            pieces.append(padded[offset_y : offset_y + out_rows, offset_x : offset_x + out_cols])
    patches = jnp.concatenate(pieces, axis=-1)
    channels = kernel.shape[-1]
    result = jnp.dot(
        patches, kernel.reshape(9 * kernel.shape[2], channels), preferred_element_type=jnp.float32
    )
    center = padded[1 : 1 + out_rows, 1 : 1 + out_cols].astype(jnp.float32)
    return (center + jax.nn.silu(result)).astype(jnp.bfloat16)


def shards(seg_feat, seg_block, depth_rank, w_in, w_hidden, w_out, w_dens, conv_w):
    block_count = lax.axis_size("blocks")
    segments = seg_feat.shape[2]
    color = render(
        block_count,
        lax.axis_size("tiles"),
        seg_feat[0, 0],
        seg_block.reshape(1, segments),
        depth_rank[0, 0],
        w_in[0],
        w_hidden[0],
        w_out[0],
        w_dens,
    )
    top, left = TH - CONV_LAYERS, TW - CONV_LAYERS
    tile_image = lax.optimization_barrier(
        color[top : 2 * TH + CONV_LAYERS, left : 2 * TW + CONV_LAYERS]
    )
    rows_total = TH * lax.axis_size(("tiles", "sub"))
    cols_total = TW * block_count
    row_pos = (
        lax.axis_index(("tiles", "sub")) * TH
        - CONV_LAYERS
        + jnp.arange(TH + 2 * CONV_LAYERS, dtype=jnp.int32)
    )
    col_pos = (
        lax.axis_index("blocks") * TW
        - CONV_LAYERS
        + jnp.arange(TW + 2 * CONV_LAYERS, dtype=jnp.int32)
    )
    inside = ((row_pos >= 0) & (row_pos < rows_total))[:, None] & (
        (col_pos >= 0) & (col_pos < cols_total)
    )[None, :]
    current = tile_image
    for layer_index in range(CONV_LAYERS):
        margin = CONV_LAYERS - layer_index - 1
        size_h = TH + 2 * margin
        size_w = TW + 2 * margin
        current = conv_layer(current, conv_w[layer_index], size_h, size_w)
        keep_mask = inside[
            layer_index + 1 : layer_index + 1 + size_h, layer_index + 1 : layer_index + 1 + size_w
        ]
        current = jnp.where(keep_mask[:, :, None], current, jnp.zeros_like(current))
    tile_image = current
    return tile_image


def solution(mesh):
    in_specs = (
        P(("groups", "tiles", "sub"), "blocks", None, None),
        P(("groups", "tiles", "sub"), "blocks", None, None),
        P(("groups", "tiles", "sub"), "blocks", None, None),
        P("blocks", None, None),
        P("blocks", None, None, None),
        P("blocks", None, None),
        P("blocks", None),
        P(),
    )
    out_specs = P(("groups", "tiles", "sub"), "blocks", None)
    return jax.shard_map(shards, mesh=mesh, in_specs=in_specs, out_specs=out_specs, check_vma=False)
```
